512 devices in a mesh: dp: 64 (over z, x, core), mp: 8 (over y).
Axes of the slice: x: 4, y: 8, z: 8, core: 2. Of those that a mesh axis runs over, the one named last changes fastest.
Arguments:
- teacher_in: bfloat16 [64, 1024, 1408], P('dp', 'mp'), may hold values from -8 to 8
- teacher_gain: float32 [1408], replicated, may hold values from 0.5 to 1.5
- teacher_qkv: bfloat16 [3, 1408, 1408], P(None, 'mp'), may hold values from -1 to 1
- teacher_out: bfloat16 [1408, 1408], P('mp'), may hold values from -0.15625 to 0.15625
- student_in: bfloat16 [64, 1024, 1024], P('dp', None, 'mp'), may hold values from -6 to 6
- student_gain: float32 [1024], replicated, may hold values from 0.25 to 1.75
- widen_weight: bfloat16 [1024, 4096], P(None, 'mp'), may hold values from -0.1875 to 0.1875
- narrow_weight: bfloat16 [4096, 1024], P('mp'), may hold values from -0.09375 to 0.09375
- target_head: bfloat16 [1408, 1024], P('mp'), may hold values from -0.1875 to 0.1875
- positions: int32 [64, 512], P('dp'), may hold values from 0 to 1023, as said below
- counts: int32 [64], P('dp'), may hold values from 1 to 512, 16384 in all
Outputs:
- grad_widen: float32 [1024, 4096], P('dp', 'mp')
- grad_narrow: float32 [1024, 4096], P('dp', 'mp')
- losses: float32 [64], P('dp')
The draws below stay inside these ranges and needn't reach their ends.
Inputs may be any that keep to these rules, and one draw needn't show every extreme that they name: `positions`: the entries of one image's list are distinct; only the first counts of them are live. The counts of all images sum to 16384.
All inputs are finite; a program needn't handle non-finite values. No bound on the sum of `counts` on one device may be relied on, other than what follows from the above.
Results may differ from the reference program's by a relative error of at most 0.02.
Values may be sent and summed in bfloat16 or wider, within the bound.
No kernel may reach another device: no remote copies, remote signals or barrier semaphores. Data moves between devices by JAX's collectives and lax.ppermute only.
A program may use at most 64 MiB of HBM per device.

```python
import math
import jax
import jax.numpy as jnp
import numpy as np
from jax import lax

TD = 1408
TH = 16
SD = 1024
SH = 4096
PATCHES = 1024
KEEP = 256
SLOTS = 512
IMAGES = 64
N_MP = 8


def draw_teacher_in(key, part):
    drawn = jax.random.normal(jax.random.fold_in(key, 13), (IMAGES, PATCHES, TD), jnp.float32)
    return jnp.clip(drawn, -6.0, 6.0).astype(jnp.bfloat16)


def draw_teacher_qkv(key, part):
    sigma = TD ** (-0.5)
    drawn = sigma * jax.random.normal(jax.random.fold_in(key, 24), (3, TD, TD), jnp.float32)
    return jnp.clip(drawn, -1.0, 1.0).astype(jnp.bfloat16)


def draw_positions(key, part):
    image_keys = jax.random.split(jax.random.fold_in(key, 31), IMAGES)
    return jax.vmap(lambda one_key: jax.random.permutation(one_key, PATCHES)[:SLOTS])(image_keys).astype(jnp.int32)


def shard_levels(rng, extent, shards, least, high):
    level = 1.0
    for axis_at, blocks in shards:
        heights = jax.random.uniform(jax.random.fold_in(jax.random.fold_in(rng, 6), axis_at), (blocks,), jnp.float32, least / len(shards), high / len(shards))
        level = level * jnp.repeat(jnp.exp(heights), extent[axis_at] // blocks).reshape((-1,) + (1,) * (len(extent) - 1 - axis_at))
    return level


def profile(count, total, limit, skew):
    loads = [(1 << 20) // math.isqrt(standing ** skew) + 1 for standing in range(2, count + 1)]
    rest, holding = total - limit - (count - 1), [1] * (count - 1)
    while rest > 0:
        candidates = [i for i in range(count - 1) if holding[i] < limit]
        mass, left = sum([loads[i] for i in candidates]), rest
        for i in candidates:
            more = min(limit - holding[i], max(1, left * loads[i] // mass), rest)
            holding[i] = holding[i] + more
            rest = rest - more
    return np.array([limit] + holding)


def uneven_parts(key, count, total, most, slope):
    if count == 2:
        one = jax.random.randint(key, (), max(1, total - most), min(most, total - 1) + 1)
        return jnp.stack([one, total - one])
    lengths = jnp.asarray(profile(count, total, most, slope), jnp.int32)
    pairs = (count - 1) // 2
    source_of, receiver = lengths[1:1 + 2 * pairs:2], lengths[2:2 + 2 * pairs:2]
    margin = jnp.minimum(source_of - 1, most - receiver)
    moved = jax.random.randint(jax.random.fold_in(key, 1), (pairs,), 0, 1 << 20) % (margin + 1)
    lengths = lengths.at[1:1 + 2 * pairs:2].set(source_of - moved).at[2:2 + 2 * pairs:2].set(receiver + moved)
    return lengths[jax.random.permutation(jax.random.fold_in(key, 2), count)]


def normal_values(key, shape, scale, limit, pieces=(), held_as=jnp.bfloat16):
    entries = scale * jax.random.normal(key, shape, jnp.float32)
    if pieces:
        entries = entries * shard_levels(key, shape, pieces, -0.22, 0.18)
    return jnp.clip(entries, -limit, limit).astype(held_as)


def setup_inputs(seed: int = 0) -> dict:
    keys = jax.random.split(jax.random.key(seed), 12)
    return {
        "teacher_in": draw_teacher_in(jax.random.fold_in(keys[11], 71), 0),
        "teacher_gain": jnp.clip(1.0 + 0.1 * jax.random.normal(keys[1], (TD,), jnp.float32), 0.5, 1.5),
        "teacher_qkv": draw_teacher_qkv(jax.random.fold_in(keys[11], 71), 0),
        "teacher_out": normal_values(keys[3], (TD, TD), TD ** -0.5, 0.15625, ((0, 8),)),
        "student_in": normal_values(keys[4], (IMAGES, PATCHES, SD), 1.0, 6.0, ((0, 64), (2, 8))),
        "student_gain": jnp.clip(1.0 + 0.15 * jax.random.normal(keys[5], (SD,), jnp.float32), 0.25, 1.75),
        "widen_weight": normal_values(keys[6], (SD, SH), SD ** -0.5, 0.1875, ((1, 8),)),
        "narrow_weight": normal_values(keys[7], (SH, SD), SH ** -0.5, 0.09375, ((0, 8),)),
        "target_head": normal_values(keys[8], (TD, SD), SD ** -0.5, 0.1875, ((0, 8),)),
        "positions": draw_positions(jax.random.fold_in(keys[11], 71), 0),
        "counts": uneven_parts(keys[10], IMAGES, IMAGES * KEEP, SLOTS, 2).astype(jnp.int32),
    }


EPSILON = 1e-06

def layer_norm(values, gain):
    mean_val = lax.optimization_barrier(jnp.mean(values, axis=-1, keepdims=True))
    centred = values - mean_val
    spread = lax.optimization_barrier(jnp.mean(centred * centred, axis=-1, keepdims=True))
    return centred * lax.rsqrt(spread + EPSILON) * gain

def gelu_value(pre):
    return 0.5 * pre * (1.0 + lax.erf(pre * 0.7071067811865476))

def gelu_slope(pre):
    return 0.5 * (1.0 + lax.erf(pre * 0.7071067811865476)) + pre * 0.3989422804014327 * jnp.exp(-0.5 * pre * pre)

def reference(teacher_in, teacher_gain, teacher_qkv, teacher_out, student_in, student_gain, widen_weight, narrow_weight, target_head, positions, counts):
    head_size = TD // TH
    factor = head_size ** (-0.5)
    hidden_block = SH // N_MP
    column_block = TD // N_MP
    narrow_blocks = narrow_weight.astype(jnp.float32).reshape(N_MP, hidden_block, SD)
    head_blocks = target_head.astype(jnp.float32).reshape(N_MP, column_block, SD)

    def one_image(running, inputs):
        acc_widen, acc_narrow = running
        patches, student_all, picked, live_count = inputs
        teach_normed = layer_norm(patches.astype(jnp.float32), teacher_gain).astype(jnp.bfloat16)
        key_rows = jnp.dot(teach_normed, teacher_qkv[1].T, preferred_element_type=jnp.float32).astype(jnp.bfloat16)
        value_rows = jnp.dot(teach_normed, teacher_qkv[2].T, preferred_element_type=jnp.float32).astype(jnp.bfloat16)
        query_rows = jnp.dot(teach_normed[picked], teacher_qkv[0].T, preferred_element_type=jnp.float32).astype(jnp.bfloat16)
        query_heads = query_rows.astype(jnp.float32).reshape(SLOTS, TH, head_size)
        key_heads = key_rows.astype(jnp.float32).reshape(PATCHES, TH, head_size)
        value_heads = value_rows.astype(jnp.float32).reshape(PATCHES, TH, head_size)
        scores = jnp.einsum('shd,phd->hsp', query_heads, key_heads) * factor
        largest = lax.optimization_barrier(jnp.max(scores, axis=-1, keepdims=True))
        soft_num = jnp.exp(scores - largest)
        soft_weights = (soft_num / lax.optimization_barrier(jnp.sum(soft_num, axis=-1, keepdims=True))).astype(jnp.bfloat16)
        attended = jnp.einsum('hsp,phd->shd', soft_weights.astype(jnp.float32), value_heads).astype(jnp.bfloat16).reshape(SLOTS, TD)
        blended = jnp.dot(attended, teacher_out.T, preferred_element_type=jnp.float32)
        targets = (patches[picked].astype(jnp.float32) + blended).astype(jnp.bfloat16)
        slot_ids = jnp.arange(SLOTS, dtype=jnp.int32)
        row_weight = jnp.where(slot_ids < live_count, 1.0 / live_count.astype(jnp.float32), jnp.zeros((), jnp.float32))
        student_rows = student_all[picked].astype(jnp.float32)
        normed_rows = layer_norm(student_rows, student_gain).astype(jnp.bfloat16)
        pre_act = jnp.dot(normed_rows, widen_weight, preferred_element_type=jnp.float32)
        activity = gelu_value(pre_act).astype(jnp.bfloat16)
        partials = jnp.einsum('smk,mkd->msd', activity.astype(jnp.float32).reshape(SLOTS, N_MP, hidden_block), narrow_blocks)
        partials = lax.optimization_barrier(partials.astype(jnp.bfloat16))
        branch_sum = lax.optimization_barrier(jnp.sum(partials.astype(jnp.float32), axis=0))
        outputs = (student_rows + branch_sum).astype(jnp.bfloat16)
        predicted = jnp.dot(outputs, target_head.T, preferred_element_type=jnp.float32)
        targets32 = targets.astype(jnp.float32)
        inner_sum = lax.optimization_barrier(jnp.sum(predicted * targets32, axis=-1))
        pred_sq = lax.optimization_barrier(jnp.sum(predicted * predicted, axis=-1))
        target_sq = lax.optimization_barrier(jnp.sum(targets32 * targets32, axis=-1))
        inv_pred = lax.rsqrt(pred_sq + EPSILON)
        inv_target = lax.rsqrt(target_sq + EPSILON)
        cosine = inner_sum * inv_pred * inv_target
        image_loss = jnp.sum(row_weight * (1.0 - cosine))
        pred_slope = (row_weight * cosine * inv_pred * inv_pred)[:, None] * predicted - (row_weight * inv_pred * inv_target)[:, None] * targets32
        pred_slope = pred_slope.astype(jnp.bfloat16)
        back_parts = jnp.einsum('smc,mcd->msd', pred_slope.astype(jnp.float32).reshape(SLOTS, N_MP, column_block), head_blocks)
        back_parts = lax.optimization_barrier(back_parts.astype(jnp.bfloat16))
        back_out = lax.optimization_barrier(jnp.sum(back_parts.astype(jnp.float32), axis=0)).astype(jnp.bfloat16)
        back_act = jnp.dot(back_out, narrow_weight.T, preferred_element_type=jnp.float32)
        back_pre = (back_act * gelu_slope(pre_act)).astype(jnp.bfloat16)
        acc_widen = acc_widen + jnp.dot(normed_rows.T, back_pre, preferred_element_type=jnp.float32)
        acc_narrow = acc_narrow + jnp.dot(back_out.T, activity, preferred_element_type=jnp.float32)
        return ((acc_widen, acc_narrow), image_loss)
    start_state = (jnp.zeros((SD, SH), jnp.float32), jnp.zeros((SD, SH), jnp.float32))
    (grad_widen, grad_narrow), losses = lax.scan(one_image, start_state, (teacher_in, student_in, positions, counts))
    return (grad_widen, grad_narrow, losses)
```

```python
import jax
import jax.numpy as jnp
from jax import lax
from jax.sharding import Mesh, PartitionSpec as P

TD = 1408
TH = 16
EPSILON = 1e-06
DP = ("z", "x", "c")
BF = jnp.bfloat16
F32 = jnp.float32


def layer_norm(values, gain):
    mean_val = jnp.mean(values, axis=-1, keepdims=True)
    centred = values - mean_val
    spread = jnp.mean(centred * centred, axis=-1, keepdims=True)
    return centred * lax.rsqrt(spread + EPSILON) * gain


def gelu_value(pre):
    return 0.5 * pre * (1.0 + lax.erf(pre * 0.7071067811865476))


def gelu_slope(pre):
    return 0.5 * (1.0 + lax.erf(pre * 0.7071067811865476)) + pre * 0.3989422804014327 * jnp.exp(
        -0.5 * pre * pre
    )


def shift(amount):
    return [(i, (i + amount) % 8) for i in range(8)]


def ring(block):
    held = [block] + [None] * 7
    right = left = block
    for step in range(1, 5):
        right = lax.ppermute(right, "mp", shift(1))
        held[step] = right
        if step < 4:
            left = lax.ppermute(left, "mp", shift(-1))
            held[8 - step] = left
    return held


def reordered(stacked, me):
    return jnp.stack(
        [lax.dynamic_index_in_dim(stacked, (me - owner) % 8, 0, False) for owner in range(8)]
    )


def to_tiles(shard, per_piece):
    rows, cols = shard.shape
    tiles = shard.reshape(rows // 8, 8, cols // 128, 128).transpose(0, 2, 1, 3)
    tiles = tiles.reshape(-1, 8, 128)
    spare = 64 * per_piece - tiles.shape[0]
    tiles = jnp.concatenate([tiles, jnp.zeros((spare, 8, 128), tiles.dtype)])
    return tiles.reshape(64, per_piece, 8, 128)


def from_tiles(pieces, rows, cols):
    count = (rows // 8) * (cols // 128)
    tiles = pieces[:, :count].reshape(8, rows // 8, cols // 128, 8, 128)
    return tiles.transpose(0, 1, 3, 2, 4).reshape(8 * rows, cols)


def on_device(
    teacher_in,
    teacher_gain,
    teacher_qkv,
    teacher_out,
    student_in,
    student_gain,
    widen_weight,
    narrow_weight,
    target_head,
    positions,
    counts,
):
    me = lax.axis_index("mp")
    at = lax.axis_index(DP)
    picked = positions[0]
    live_count = counts[0]
    head = TD // TH
    factor = head ** (-0.5)

    mine = jnp.concatenate(
        [
            lax.dynamic_index_in_dim(to_tiles(teacher_out, 4), at, 0, False),
            lax.dynamic_index_in_dim(to_tiles(target_head, 3), at, 0, False),
        ]
    )
    shares = lax.all_to_all(
        jnp.broadcast_to(mine, (8, *mine.shape)), "mp", 0, 0, tiled=True
    )
    out_full = from_tiles(lax.all_gather(shares[:, :4], DP, axis=1, tiled=True), 176, 1408)
    head_full = from_tiles(lax.all_gather(shares[:, 4:], DP, axis=1, tiled=True), 176, 1024)

    rows = student_in[0][picked]
    packed = jnp.concatenate([rows[128 * g : 128 * g + 128] for g in range(4)], axis=1)
    held = ring(jnp.concatenate([teacher_in[0], packed], axis=1))

    stacked = jnp.stack([h[:, TD:] for h in held])
    by_owner = reordered(stacked, me).reshape(8, 128, 4, 128)
    student = by_owner.transpose(2, 1, 0, 3).reshape(512, 1024)
    normed_rows = layer_norm(student.astype(F32), student_gain).astype(BF)
    pre_act = jnp.dot(normed_rows, widen_weight, preferred_element_type=F32)
    activity = gelu_value(pre_act).astype(BF)
    partial = jnp.dot(activity, narrow_weight, preferred_element_type=F32).astype(BF)
    arrived = lax.all_to_all(partial.reshape(8, 64, 1024), "mp", 0, 0, tiled=True)
    branch = jnp.sum(arrived.astype(F32), axis=0)
    own_rows = lax.dynamic_slice_in_dim(student, me * 64, 64, 0)
    outputs = (own_rows.astype(F32) + branch).astype(BF)

    weights = jnp.pad(teacher_qkv.reshape(3, 2, head, TD), ((0, 0), (0, 0), (0, 128 - head), (0, 0)))
    weights = weights.reshape(768, TD)
    made = []
    for h in held:
        normed = layer_norm(h[:, :TD].astype(F32), teacher_gain).astype(BF)
        made.append(
            jnp.einsum("pi,oi->po", normed, weights, preferred_element_type=F32).astype(BF)
        )
    made = jnp.concatenate(made)
    place = ((me - picked // 128) % 8) * 128 + picked % 128
    query = made[:, :256][place].reshape(512, 2, 128)
    key = made[:, 256:512].reshape(1024, 2, 128)
    value = made[:, 512:].reshape(1024, 2, 128)
    scores = jnp.einsum("shd,phd->hsp", query, key, preferred_element_type=F32) * factor
    soft_num = jnp.exp(scores - jnp.max(scores, axis=-1, keepdims=True))
    soft = (soft_num / jnp.sum(soft_num, axis=-1, keepdims=True)).astype(BF)
    attended = jnp.einsum("hsp,phd->shd", soft, value, preferred_element_type=F32)
    attended = attended[:, :, :head].astype(BF).reshape(8, 64, 176)
    attended = lax.all_to_all(attended, "mp", 0, 0, tiled=True)
    attended = attended.transpose(1, 0, 2).reshape(64, TD)
    own_place = lax.dynamic_slice_in_dim(place, me * 64, 64, 0)
    patches = jnp.concatenate([h[:, :TD] for h in held])
    blended = jnp.einsum("sw,ow->so", attended, out_full, preferred_element_type=F32)
    targets = (patches[own_place].astype(F32) + blended).astype(BF).astype(F32)

    slot = me * 64 + jnp.arange(64, dtype=jnp.int32)
    row_weight = jnp.where(slot < live_count, 1.0 / live_count.astype(F32), jnp.zeros((), F32))
    predicted = jnp.einsum("rd,cd->rc", outputs, head_full, preferred_element_type=F32)
    inner = jnp.sum(predicted * targets, axis=-1)
    inv_pred = lax.rsqrt(jnp.sum(predicted * predicted, axis=-1) + EPSILON)
    inv_target = lax.rsqrt(jnp.sum(targets * targets, axis=-1) + EPSILON)
    cosine = inner * inv_pred * inv_target
    row_loss = row_weight * (1.0 - cosine)
    slope = (row_weight * cosine * inv_pred * inv_pred)[:, None] * predicted - (
        row_weight * inv_pred * inv_target
    )[:, None] * targets
    back_own = jnp.dot(slope.astype(BF), head_full, preferred_element_type=F32).astype(BF)
    loss_high = row_loss.astype(BF)
    loss_low = (row_loss - loss_high.astype(F32)).astype(BF)
    extra = jnp.pad(jnp.stack([loss_high, loss_low], axis=1), ((0, 0), (0, 126)))
    back_held = jnp.stack(ring(jnp.concatenate([back_own, extra], axis=1)))
    back_held = reordered(back_held, me).reshape(512, 1152)
    image_loss = jnp.sum(back_held[:, 1024:].astype(F32))
    back = back_held[:, :1024]

    back_act = jnp.einsum("rd,hd->rh", back, narrow_weight, preferred_element_type=F32)
    back_pre = (back_act * gelu_slope(pre_act)).astype(BF)
    grad_w = jnp.einsum("rd,rh->dh", normed_rows, back_pre, preferred_element_type=F32)
    grad_n = jnp.einsum("rd,rh->dh", back, activity, preferred_element_type=F32)
    grads = jnp.concatenate(
        [grad_w.astype(BF).reshape(32, 2, 16, 512), grad_n.astype(BF).reshape(32, 2, 16, 512)], 2
    )
    core = lax.axis_index("c")
    other = lax.ppermute(
        lax.dynamic_index_in_dim(grads, 1 - core, 1, False), "c", [(0, 1), (1, 0)]
    )
    kept = lax.dynamic_index_in_dim(grads, core, 1, False).astype(F32) + other.astype(F32)
    kept = kept.astype(BF).reshape(8, 4, 32, 512)
    kept = lax.all_to_all(kept, "x", 1, 0, tiled=False)
    kept = jnp.sum(kept.astype(F32), axis=0).astype(BF)
    kept = lax.all_to_all(kept, "z", 0, 0, tiled=True)
    total = jnp.sum(kept.astype(F32), axis=0)
    return (total[:16], total[16:], jnp.reshape(image_loss, (1,)))


def solution(mesh):
    grid = Mesh(mesh.devices.reshape(8, 4, 2, 8), ("z", "x", "c", "mp"))
    placed = (
        P(DP, "mp", None),
        P(),
        P(None, "mp", None),
        P("mp", None),
        P(DP, None, "mp"),
        P(),
        P(None, "mp"),
        P("mp", None),
        P("mp", None),
        P(DP, None),
        P(DP),
    )
    return jax.shard_map(
        on_device,
        mesh=grid,
        in_specs=placed,
        out_specs=(P(DP, "mp"), P(DP, "mp"), P(DP)),
        check_vma=False,
    )
```

```python
import jax
import jax.numpy as jnp
from jax import lax
from jax.experimental import pallas as pl
from jax.experimental.pallas import tpu as pltpu
from jax.sharding import Mesh, PartitionSpec as P

TD = 1408
TH = 16
EPSILON = 1e-06
DP = ("z", "x", "c")
BF = jnp.bfloat16
F32 = jnp.float32


def layer_norm(values, gain):
    mean_val = jnp.mean(values, axis=-1, keepdims=True)
    centred = values - mean_val
    spread = jnp.mean(centred * centred, axis=-1, keepdims=True)
    return centred * lax.rsqrt(spread + EPSILON) * gain


def shift(amount):
    return [(i, (i + amount) % 8) for i in range(8)]


def ring(block):
    held = [block] + [None] * 7
    right = left = block
    for step in range(1, 5):
        right = lax.ppermute(right, "mp", shift(1))
        held[step] = right
        if step < 4:
            left = lax.ppermute(left, "mp", shift(-1))
            held[8 - step] = left
    return held


def reordered(stacked, me):
    return jnp.stack(
        [lax.dynamic_index_in_dim(stacked, (me - owner) % 8, 0, False) for owner in range(8)]
    )


def to_tiles(shard, per_piece):
    rows, cols = shard.shape
    tiles = shard.reshape(rows // 8, 8, cols // 128, 128).transpose(0, 2, 1, 3)
    tiles = tiles.reshape(-1, 8, 128)
    spare = 64 * per_piece - tiles.shape[0]
    tiles = jnp.concatenate([tiles, jnp.zeros((spare, 8, 128), tiles.dtype)])
    return tiles.reshape(64, per_piece, 8, 128)


def from_tiles(pieces, rows, cols):
    count = (rows // 8) * (cols // 128)
    tiles = pieces[:, :count].reshape(8, rows // 8, cols // 128, 8, 128)
    return tiles.transpose(0, 1, 3, 2, 4).reshape(8 * rows, cols)


VMEM = pl.BlockSpec(memory_space=pltpu.VMEM)
SMEM = pl.BlockSpec(memory_space=pltpu.SMEM)
LANES = (((1,), (1,)), ((), ()))


def kernel_call(body, outs, scratch=(), flops=0, scalars=0, arrays=0, moved=0, limit=32):
    return pl.pallas_call(
        body,
        out_shape=outs,
        in_specs=[SMEM] * scalars + [VMEM] * arrays,
        out_specs=[VMEM] * len(outs),
        scratch_shapes=scratch,
        compiler_params=pltpu.CompilerParams(vmem_limit_bytes=limit << 20),
        cost_estimate=pl.CostEstimate(flops=flops, bytes_accessed=moved, transcendentals=0),
    )


def project_body(block, gain, weights, made):
    values = block[:, :TD].astype(F32)
    normed = layer_norm(values, gain[...]).astype(BF)
    gap = jnp.zeros((128, 40), F32)
    for j in range(3):
        part = lax.dot_general(normed, weights[j], LANES, preferred_element_type=F32)
        part = jnp.concatenate([part[:, :88], gap, part[:, 88:], gap], axis=1)
        made[:, 256 * j : 256 * j + 256] = part.astype(BF)


def project(block, gain, weights):
    return kernel_call(
        project_body,
        [jax.ShapeDtypeStruct((128, 768), BF)],
        flops=2 * 128 * 528 * TD,
        arrays=3,
        moved=2_500_000,
    )(block, gain, weights)[0]


def attend_body(place, *refs):
    made, out = refs[:8], refs[8]
    keys, values, queries = refs[9:]
    for s in range(8):
        queries[128 * s : 128 * s + 128, :] = made[s][:, :256]
        keys[128 * s : 128 * s + 128, :] = made[s][:, 256:512]
        values[128 * s : 128 * s + 128, :] = made[s][:, 512:]

    def chunk(i, _):
        rows = pl.ds(pl.multiple_of(i * 128, 128), 128)
        spots = lax.broadcasted_iota(jnp.int32, (128, 1024), 1)
        chosen = jnp.where(spots == place[rows, :], 1.0, 0.0).astype(BF)
        query = jnp.dot(chosen, queries[...], preferred_element_type=F32).astype(BF)
        heads = []
        for h in range(2):
            lanes = slice(128 * h, 128 * h + 128)
            scores = lax.dot_general(
                query[:, lanes], keys[:, lanes], LANES, preferred_element_type=F32
            ) * ((TD // TH) ** (-0.5))
            top = jnp.max(scores, axis=-1, keepdims=True)
            num = jnp.exp(scores - top)
            soft = (num * (1.0 / jnp.sum(num, axis=-1, keepdims=True))).astype(BF)
            heads.append(jnp.dot(soft, values[:, lanes], preferred_element_type=F32)[:, :88])
        out[rows, :] = jnp.concatenate(heads, axis=1).astype(BF)
        return 0

    lax.fori_loop(0, 4, chunk, 0)


def attend(place, made):
    return kernel_call(
        attend_body,
        [jax.ShapeDtypeStruct((512, 176), BF)],
        scratch=[pltpu.VMEM((1024, 256), BF)] * 3,
        flops=2 * 512 * 1024 * (256 + 256 + 256),
        arrays=9,
        moved=4_000_000,
    )(place, *made)[0]


def pick_body(place, *refs):
    held, out = refs[:8], refs[8]
    spots = lax.broadcasted_iota(jnp.int32, (64, 128), 1)
    total = jnp.zeros((64, TD), F32)
    for s in range(8):
        chosen = jnp.where(spots + 128 * s == place[...], 1.0, 0.0).astype(BF)
        total += jnp.dot(chosen, held[s][:, :TD], preferred_element_type=F32)
    out[...] = total.astype(BF)


def pick(place, held):
    return kernel_call(
        pick_body,
        [jax.ShapeDtypeStruct((64, TD), BF)],
        flops=2 * 64 * 1024 * TD,
        arrays=9,
        moved=4_000_000,
    )(place, *held)[0]


def forward_body(me_ref, *refs):
    held, (gain, widen, narrow) = refs[:8], refs[8:11]
    normed_out, active_out, slope_out, partial_out, own_out, rows_by = refs[11:]
    me = me_ref[0]
    for s in range(8):
        owner = lax.rem(me + (8 - s), 8)
        for g in range(4):
            rows_by[owner, 128 * g : 128 * g + 128, :] = held[s][
                :, TD + 128 * g : TD + 128 * g + 128
            ]
    mine = pl.ds(pl.multiple_of(me * 64, 64), 64)
    for b in range(8):
        own_out[:, 128 * b : 128 * b + 128] = rows_by[b, mine, :]

    def chunk(i, _):
        rows = pl.ds(pl.multiple_of(i * 128, 128), 128)
        values = jnp.concatenate([rows_by[b, rows, :] for b in range(8)], axis=1).astype(F32)
        normed = layer_norm(values, gain[...]).astype(BF)
        normed_out[rows, :] = normed
        pre = jnp.dot(normed, widen[...], preferred_element_type=F32)
        half = 0.5 * (1.0 + lax.erf(pre * 0.7071067811865476))
        active = (pre * half).astype(BF)
        active_out[rows, :] = active
        slope_out[rows, :] = half + pre * 0.3989422804014327 * jnp.exp(-0.5 * pre * pre)
        partial_out[rows, :] = jnp.dot(active, narrow[...], preferred_element_type=F32).astype(BF)
        return 0

    lax.fori_loop(0, 4, chunk, 0)


def forward(me, held, gain, widen, narrow):
    return kernel_call(
        forward_body,
        [
            jax.ShapeDtypeStruct((512, 1024), BF),
            jax.ShapeDtypeStruct((512, 512), BF),
            jax.ShapeDtypeStruct((512, 512), F32),
            jax.ShapeDtypeStruct((512, 1024), BF),
            jax.ShapeDtypeStruct((64, 1024), BF),
        ],
        scratch=[pltpu.VMEM((8, 512, 128), BF)],
        flops=4 * 512 * 1024 * 512,
        scalars=1,
        arrays=11,
        moved=6_000_000,
    )(me, *held, gain, widen, narrow)


def loss_body(weight, arrived, own, attended, picked, out_full, head_full, back_out):
    branch = arrived[0].astype(F32)
    for b in range(1, 8):
        branch += arrived[b].astype(F32)
    outputs = (own[...].astype(F32) + branch).astype(BF)
    joined = jnp.concatenate([attended[b].astype(F32) for b in range(8)], axis=1).astype(BF)
    blended = lax.dot_general(joined, out_full[...], LANES, preferred_element_type=F32)
    targets = (picked[...].astype(F32) + blended).astype(BF).astype(F32)
    predicted = lax.dot_general(outputs, head_full[...], LANES, preferred_element_type=F32)
    inner = jnp.sum(predicted * targets, axis=-1, keepdims=True)
    inv_pred = lax.rsqrt(jnp.sum(predicted * predicted, axis=-1, keepdims=True) + EPSILON)
    inv_target = lax.rsqrt(jnp.sum(targets * targets, axis=-1, keepdims=True) + EPSILON)
    cosine = inner * inv_pred * inv_target
    row_weight = weight[...]
    slope = (row_weight * cosine * inv_pred * inv_pred) * predicted - (
        row_weight * inv_pred * inv_target
    ) * targets
    back = jnp.dot(slope.astype(BF), head_full[...], preferred_element_type=F32)
    back_out[:, :1024] = back.astype(BF)
    row_loss = row_weight * (1.0 - cosine)
    high = row_loss.astype(BF).astype(F32)
    lane = lax.broadcasted_iota(jnp.int32, (64, 128), 1)
    extra = jnp.where(lane == 0, high, jnp.where(lane == 1, row_loss - high, 0.0))
    back_out[:, 1024:] = extra.astype(BF)


def loss_step(weight, arrived, own, attended, picked, out_full, head_full):
    return kernel_call(
        loss_body,
        [jax.ShapeDtypeStruct((64, 1152), BF)],
        flops=2 * 64 * 1408 * (1408 + 2048),
        arrays=7,
        moved=10_000_000,
    )(weight, arrived, own, attended, picked, out_full, head_full)[0]


def on_device(
    teacher_in,
    teacher_gain,
    teacher_qkv,
    teacher_out,
    student_in,
    student_gain,
    widen_weight,
    narrow_weight,
    target_head,
    positions,
    counts,
):
    me = lax.axis_index("mp")
    at = lax.axis_index(DP)
    picked = positions[0]
    live_count = counts[0]
    head = TD // TH
    factor = head ** (-0.5)

    mine = jnp.concatenate(
        [
            lax.dynamic_index_in_dim(to_tiles(teacher_out, 4), at, 0, False),
            lax.dynamic_index_in_dim(to_tiles(target_head, 3), at, 0, False),
        ]
    )
    shares = lax.all_to_all(
        jnp.broadcast_to(mine, (8, *mine.shape)), "mp", 0, 0, tiled=True
    )
    pieces = lax.all_gather(shares, DP, axis=0).reshape(64, 8, 7, 8, 128).transpose(1, 0, 2, 3, 4)
    out_full = from_tiles(pieces[:, :, :4].reshape(8, 256, 8, 128), 176, 1408)
    head_full = from_tiles(pieces[:, :, 4:].reshape(8, 192, 8, 128), 176, 1024)

    rows = student_in[0][picked]
    packed = jnp.concatenate([rows[128 * g : 128 * g + 128] for g in range(4)], axis=1)
    held = ring(jnp.concatenate([teacher_in[0], packed], axis=1))

    here = jnp.reshape(me, (1,)).astype(jnp.int32)
    normed_rows, activity, slope_pre, partial, own_rows = forward(
        here, held, student_gain.reshape(1, -1), widen_weight, narrow_weight
    )
    arrived = lax.all_to_all(partial.reshape(8, 64, 1024), "mp", 0, 0, tiled=True)

    made = [project(h, teacher_gain.reshape(1, -1), teacher_qkv) for h in held]
    place = ((me - picked // 128) % 8) * 128 + picked % 128
    attended = attend(place.reshape(512, 1), made)
    attended = lax.all_to_all(attended.reshape(8, 64, 176), "mp", 0, 0, tiled=True)
    own_place = lax.dynamic_slice_in_dim(place, me * 64, 64, 0)
    own_patches = pick(own_place.reshape(64, 1), held)

    slot = me * 64 + jnp.arange(64, dtype=jnp.int32)
    row_weight = jnp.where(slot < live_count, 1.0 / live_count.astype(F32), jnp.zeros((), F32))
    back_own = loss_step(
        row_weight.reshape(64, 1), arrived, own_rows, attended, own_patches, out_full, head_full
    )
    back_held = jnp.stack(ring(back_own))
    back_held = reordered(back_held, me).reshape(512, 1152)
    image_loss = jnp.sum(back_held[:, 1024:].astype(F32))
    back = back_held[:, :1024]

    back_act = jnp.einsum("rd,hd->rh", back, narrow_weight, preferred_element_type=F32)
    back_pre = (back_act * slope_pre).astype(BF)
    grad_w = jnp.einsum("rd,rh->dh", normed_rows, back_pre, preferred_element_type=F32)
    grad_n = jnp.einsum("rd,rh->dh", back, activity, preferred_element_type=F32)
    grads = jnp.concatenate(
        [grad_w.astype(BF).reshape(32, 2, 16, 512), grad_n.astype(BF).reshape(32, 2, 16, 512)], 2
    )
    core = lax.axis_index("c")
    other = lax.ppermute(
        lax.dynamic_index_in_dim(grads, 1 - core, 1, False), "c", [(0, 1), (1, 0)]
    )
    kept = lax.dynamic_index_in_dim(grads, core, 1, False).astype(F32) + other.astype(F32)
    kept = kept.astype(BF).reshape(8, 4, 32, 512)
    kept = lax.all_to_all(kept, "x", 1, 0, tiled=False)
    kept = jnp.sum(kept.astype(F32), axis=0).astype(BF)
    kept = lax.all_to_all(kept, "z", 0, 0, tiled=True)
    total = jnp.sum(kept.astype(F32), axis=0)
    return (total[:16], total[16:], jnp.reshape(image_loss, (1,)))


def solution(mesh):
    grid = Mesh(mesh.devices.reshape(8, 4, 2, 8), ("z", "x", "c", "mp"))
    placed = (
        P(DP, "mp", None),
        P(),
        P(None, "mp", None),
        P("mp", None),
        P(DP, None, "mp"),
        P(),
        P(None, "mp"),
        P("mp", None),
        P("mp", None),
        P(DP, None),
        P(DP),
    )
    return jax.shard_map(
        on_device,
        mesh=grid,
        in_specs=placed,
        out_specs=(P(DP, "mp"), P(DP, "mp"), P(DP)),
        check_vma=False,
    )
```

```python
import jax
import jax.numpy as jnp
from jax import lax
from jax.experimental import pallas as pl
from jax.experimental.pallas import tpu as pltpu
from jax.sharding import Mesh, PartitionSpec as P

TD = 1408
TH = 16
EPSILON = 1e-06
DP = ("z", "x", "c")
BF = jnp.bfloat16
F32 = jnp.float32


def layer_norm(values, gain):
    mean_val = jnp.mean(values, axis=-1, keepdims=True)
    centred = values - mean_val
    spread = jnp.mean(centred * centred, axis=-1, keepdims=True)
    return centred * lax.rsqrt(spread + EPSILON) * gain


def shift(amount):
    return [(i, (i + amount) % 8) for i in range(8)]


def ring(block):
    held = [block] + [None] * 7
    right = left = block
    for step in range(1, 5):
        right = lax.ppermute(right, "mp", shift(1))
        held[step] = right
        if step < 4:
            left = lax.ppermute(left, "mp", shift(-1))
            held[8 - step] = left
    return held


def to_tiles(shard, per_piece):
    rows, cols = shard.shape
    tiles = shard.reshape(rows // 16, 16, cols // 128, 128).transpose(0, 2, 1, 3)
    tiles = tiles.reshape(-1, 16, 128)
    spare = 16 * per_piece - tiles.shape[0]
    tiles = jnp.concatenate([tiles, jnp.zeros((spare, 16, 128), tiles.dtype)])
    return tiles.reshape(16, per_piece, 16, 128)


VMEM = pl.BlockSpec(memory_space=pltpu.VMEM)
SMEM = pl.BlockSpec(memory_space=pltpu.SMEM)
LANES = (((1,), (1,)), ((), ()))


def kernel_call(body, outs, scratch=(), flops=0, scalars=0, arrays=0, moved=0, limit=8):
    return pl.pallas_call(
        body,
        out_shape=outs,
        in_specs=[SMEM] * scalars + [VMEM] * arrays,
        out_specs=[VMEM] * len(outs),
        scratch_shapes=scratch,
        compiler_params=pltpu.CompilerParams(vmem_limit_bytes=limit << 20),
        cost_estimate=pl.CostEstimate(flops=flops, bytes_accessed=moved, transcendentals=0),
    )


def project_body(block, gain, weights, made):
    values = block[:, :TD].astype(F32)
    normed = layer_norm(values, gain[...]).astype(BF)
    gap = jnp.zeros((128, 40), F32)
    for j in range(3):
        part = lax.dot_general(normed, weights[j], LANES, preferred_element_type=F32)
        part = jnp.concatenate([part[:, :88], gap, part[:, 88:], gap], axis=1)
        made[:, 256 * j : 256 * j + 256] = part.astype(BF)


def project(block, gain, weights):
    return kernel_call(
        project_body,
        [jax.ShapeDtypeStruct((128, 768), BF)],
        flops=2 * 128 * 528 * TD,
        arrays=3,
        moved=2_500_000,
    )(block, gain, weights)[0]


def middle_body(me_ref, *refs):
    held, made, (place, gain, widen, narrow) = refs[:8], refs[8:16], refs[16:20]
    normed_out, active_out, slope_out, joint, own_out, picked_out = refs[20:26]
    rows_by, queries, keys, values = refs[26:]
    me = me_ref[0]
    mine = pl.ds(pl.multiple_of(me * 64, 64), 64)

    for s in range(8):
        owner = lax.rem(me + (8 - s), 8)
        for g in range(4):
            rows_by[owner, 128 * g : 128 * g + 128, :] = held[s][
                :, TD + 128 * g : TD + 128 * g + 128
            ]
    for b in range(8):
        own_out[:, 128 * b : 128 * b + 128] = rows_by[b, mine, :]

    spots = lax.broadcasted_iota(jnp.int32, (64, 128), 1)
    own_place = place[mine, :]
    total = jnp.zeros((64, TD), F32)
    for s in range(8):
        chosen = jnp.where(spots + 128 * s == own_place, 1.0, 0.0).astype(BF)
        total += jnp.dot(chosen, held[s][:, :TD], preferred_element_type=F32)
    picked_out[...] = total.astype(BF)

    for s in range(8):
        queries[128 * s : 128 * s + 128, :] = made[s][:, :256]
        keys[128 * s : 128 * s + 128, :] = made[s][:, 256:512]
        values[128 * s : 128 * s + 128, :] = made[s][:, 512:]

    def chunk(i, _):
        rows = pl.ds(pl.multiple_of(i * 128, 128), 128)
        student = jnp.concatenate([rows_by[b, rows, :] for b in range(8)], axis=1).astype(F32)
        normed = layer_norm(student, gain[...]).astype(BF)
        normed_out[rows, :] = normed
        pre = jnp.dot(normed, widen[...], preferred_element_type=F32)
        half = 0.5 * (1.0 + lax.erf(pre * 0.7071067811865476))
        active = (pre * half).astype(BF)
        active_out[rows, :] = active
        slope_out[rows, :] = half + pre * 0.3989422804014327 * jnp.exp(-0.5 * pre * pre)
        joint[rows, :1024] = jnp.dot(active, narrow[...], preferred_element_type=F32).astype(BF)

        spots = lax.broadcasted_iota(jnp.int32, (128, 1024), 1)
        chosen = jnp.where(spots == place[rows, :], 1.0, 0.0).astype(BF)
        query = jnp.dot(chosen, queries[...], preferred_element_type=F32).astype(BF)
        heads = []
        for h in range(2):
            lanes = slice(128 * h, 128 * h + 128)
            scores = lax.dot_general(
                query[:, lanes], keys[:, lanes], LANES, preferred_element_type=F32
            ) * ((TD // TH) ** (-0.5))
            top = jnp.max(scores, axis=-1, keepdims=True)
            num = jnp.exp(scores - top)
            soft = (num * (1.0 / jnp.sum(num, axis=-1, keepdims=True))).astype(BF)
            heads.append(jnp.dot(soft, values[:, lanes], preferred_element_type=F32)[:, :88])
        heads.append(jnp.zeros((128, 80), F32))
        joint[rows, 1024:] = jnp.concatenate(heads, axis=1).astype(BF)
        return 0

    lax.fori_loop(0, 4, chunk, 0)


def middle(me, held, made, place, gain, widen, narrow):
    return kernel_call(
        middle_body,
        [
            jax.ShapeDtypeStruct((512, 1024), BF),
            jax.ShapeDtypeStruct((512, 512), BF),
            jax.ShapeDtypeStruct((512, 512), F32),
            jax.ShapeDtypeStruct((512, 1280), BF),
            jax.ShapeDtypeStruct((64, 1024), BF),
            jax.ShapeDtypeStruct((64, TD), BF),
        ],
        scratch=[pltpu.VMEM((8, 512, 128), BF)] + [pltpu.VMEM((1024, 256), BF)] * 3,
        flops=2 * 512 * 1024 * (1024 + 768) + 2 * 64 * 1024 * TD,
        scalars=1,
        arrays=20,
        moved=12_000_000,
        limit=12,
    )(me, *held, *made, place, gain, widen, narrow)


def loss_body(weight, arrived, own, picked, out_full, head_full, back_out):
    branch = arrived[0, :, :1024].astype(F32)
    for b in range(1, 8):
        branch += arrived[b, :, :1024].astype(F32)
    outputs = (own[...].astype(F32) + branch).astype(BF)
    joined = jnp.concatenate([arrived[b, :, 1024:].astype(F32)[:, :176] for b in range(8)], axis=1).astype(BF)
    blended = lax.dot_general(joined, out_full[...], LANES, preferred_element_type=F32)
    targets = (picked[...].astype(F32) + blended).astype(BF).astype(F32)
    predicted = lax.dot_general(outputs, head_full[...], LANES, preferred_element_type=F32)
    inner = jnp.sum(predicted * targets, axis=-1, keepdims=True)
    inv_pred = lax.rsqrt(jnp.sum(predicted * predicted, axis=-1, keepdims=True) + EPSILON)
    inv_target = lax.rsqrt(jnp.sum(targets * targets, axis=-1, keepdims=True) + EPSILON)
    cosine = inner * inv_pred * inv_target
    row_weight = weight[...]
    slope = (row_weight * cosine * inv_pred * inv_pred) * predicted - (
        row_weight * inv_pred * inv_target
    ) * targets
    back = jnp.dot(slope.astype(BF), head_full[...], preferred_element_type=F32).astype(BF)
    loss = jnp.sum(row_weight * (1.0 - cosine), axis=0, keepdims=True)
    high = loss.astype(BF).astype(F32)
    lane = lax.broadcasted_iota(jnp.int32, (16, 128), 1)
    row = lax.broadcasted_iota(jnp.int32, (16, 128), 0)
    extra = jnp.where(lane == 0, high, jnp.where(lane == 1, loss - high, 0.0))
    extra = jnp.where(row == 0, extra, 0.0).astype(BF)
    for peer in range(8):
        for t in range(32):
            r, c = 16 * (t // 8), 128 * (t % 8)
            back_out[peer, t] = back[r : r + 16, c : c + 128]
        back_out[peer, 32] = extra


def loss_step(weight, arrived, own, picked, out_full, head_full):
    return kernel_call(
        loss_body,
        [jax.ShapeDtypeStruct((8, 33, 16, 128), BF)],
        flops=2 * 64 * 1408 * (1408 + 2048),
        arrays=6,
        moved=10_000_000,
    )(weight, arrived, own, picked, out_full, head_full)[0]


def assemble_body(pieces, out_full, head_full):
    def shard(y, _):
        for t in range(121):
            rows = pl.ds(pl.multiple_of(y * 176 + 16 * (t // 11), 16), 16)
            col = 128 * (t % 11)
            out_full[rows, col : col + 128] = pieces[t // 8, y, t % 8]
        for t in range(88):
            rows = pl.ds(pl.multiple_of(y * 176 + 16 * (t // 8), 16), 16)
            col = 128 * (t % 8)
            head_full[rows, col : col + 128] = pieces[t // 6, y, 8 + t % 6]
        return 0

    lax.fori_loop(0, 8, shard, 0)


def assemble(pieces):
    return kernel_call(
        assemble_body,
        [jax.ShapeDtypeStruct((TD, TD), BF), jax.ShapeDtypeStruct((TD, 1024), BF)],
        arrays=1,
        moved=14_000_000,
    )(pieces)


def tail_body(core_ref, back_in, normed, active, slope, narrow, keep, send, loss, back, pre):
    core = core_ref[0]
    for y in range(8):
        for t in range(32):
            r, c = 64 * y + 16 * (t // 8), 128 * (t % 8)
            back[r : r + 16, c : c + 128] = back_in[y, t]
    total = back_in[0, 32].astype(F32)
    for y in range(1, 8):
        total += back_in[y, 32].astype(F32)
    loss[0] = jnp.sum(total)

    def rows_chunk(i, _):
        rows = pl.ds(pl.multiple_of(i * 128, 128), 128)
        got = lax.dot_general(back[rows, :], narrow[...], LANES, preferred_element_type=F32)
        pre[rows, :] = (got * slope[rows, :]).astype(BF)
        return 0

    lax.fori_loop(0, 4, rows_chunk, 0)
    over_rows = (((0,), (0,)), ((), ()))

    def column_chunk(j, _):
        cols = pl.ds(pl.multiple_of(j * 128, 128), 128)
        grad_w = lax.dot_general(
            normed[:, cols], pre[...], over_rows, preferred_element_type=F32
        ).astype(BF)
        grad_n = lax.dot_general(
            back[:, cols], active[...], over_rows, preferred_element_type=F32
        ).astype(BF)

        def put(even, odd):
            for q in range(8):
                target = odd if q % 2 else even
                target[4 * j + q // 2, :16, :] = grad_w[16 * q : 16 * q + 16]
                target[4 * j + q // 2, 16:, :] = grad_n[16 * q : 16 * q + 16]

        pl.when(core == 0)(lambda: put(keep, send))
        pl.when(core == 1)(lambda: put(send, keep))
        return 0

    lax.fori_loop(0, 8, column_chunk, 0)


def tail(core, back, normed, active, slope, narrow):
    half = jax.ShapeDtypeStruct((32, 32, 512), BF)
    return pl.pallas_call(
        tail_body,
        out_shape=[half, half, jax.ShapeDtypeStruct((1,), F32)],
        in_specs=[SMEM] + [VMEM] * 5,
        out_specs=[VMEM, VMEM, SMEM],
        scratch_shapes=[pltpu.VMEM((512, 1024), BF), pltpu.VMEM((512, 512), BF)],
        compiler_params=pltpu.CompilerParams(vmem_limit_bytes=12 << 20),
        cost_estimate=pl.CostEstimate(
            flops=6 * 512 * 1024 * 512, bytes_accessed=8_000_000, transcendentals=0
        ),
    )(core, back, normed, active, slope, narrow)


def on_device(
    teacher_in,
    teacher_gain,
    teacher_qkv,
    teacher_out,
    student_in,
    student_gain,
    widen_weight,
    narrow_weight,
    target_head,
    positions,
    counts,
):
    me = lax.axis_index("mp")
    picked = positions[0]
    live_count = counts[0]

    rows = student_in[0][picked]
    packed = jnp.concatenate([rows[128 * g : 128 * g + 128] for g in range(4)], axis=1)
    held = ring(jnp.concatenate([teacher_in[0], packed], axis=1))

    at = lax.axis_index(("z", "c"))
    mine = jnp.concatenate(
        [
            lax.dynamic_index_in_dim(to_tiles(teacher_out, 8), at, 0, False),
            lax.dynamic_index_in_dim(to_tiles(target_head, 6), at, 0, False),
        ]
    )
    shares = lax.all_to_all(
        jnp.broadcast_to(mine, (8, *mine.shape)), "mp", 0, 0, tiled=True
    )
    shares, _, _ = lax.optimization_barrier((shares, held[1], held[7]))
    out_full, head_full = assemble(lax.all_gather(shares, ("z", "c"), axis=0))

    here = jnp.reshape(me, (1,)).astype(jnp.int32)
    made = [project(h, teacher_gain.reshape(1, -1), teacher_qkv) for h in held]
    place = ((me - picked // 128) % 8) * 128 + picked % 128
    normed_rows, activity, slope_pre, joint, own_rows, own_patches = middle(
        here,
        held,
        made,
        place.reshape(512, 1),
        student_gain.reshape(1, -1),
        widen_weight,
        narrow_weight,
    )
    arrived = lax.all_to_all(joint.reshape(8, 64, 1280), "mp", 0, 0, tiled=True)

    slot = me * 64 + jnp.arange(64, dtype=jnp.int32)
    row_weight = jnp.where(slot < live_count, 1.0 / live_count.astype(F32), jnp.zeros((), F32))
    back_own = loss_step(
        row_weight.reshape(64, 1), arrived, own_rows, own_patches, out_full, head_full
    )
    back = lax.all_to_all(back_own, "mp", 0, 0, tiled=True)

    core = jnp.reshape(lax.axis_index("c"), (1,)).astype(jnp.int32)
    keep, send, image_loss = tail(core, back, normed_rows, activity, slope_pre, narrow_weight)
    other = lax.ppermute(send, "c", [(0, 1), (1, 0)])
    kept = (keep.astype(F32) + other.astype(F32)).astype(BF)
    kept = lax.all_to_all(kept, ("z", "x"), 0, 0, tiled=True)
    total = jnp.sum(kept.astype(F32), axis=0)
    return (total[:16], total[16:], image_loss)


def solution(mesh):
    grid = Mesh(mesh.devices.reshape(8, 4, 2, 8), ("z", "x", "c", "mp"))
    placed = (
        P(DP, "mp", None),
        P(),
        P(None, "mp", None),
        P("mp", None),
        P(DP, None, "mp"),
        P(),
        P(None, "mp"),
        P("mp", None),
        P("mp", None),
        P(DP, None),
        P(DP),
    )
    return jax.shard_map(
        on_device,
        mesh=grid,
        in_specs=placed,
        out_specs=(P(DP, "mp"), P(DP, "mp"), P(DP)),
        check_vma=False,
    )
```

```python
import jax
import jax.numpy as jnp
from jax import lax
from jax.experimental import pallas as pl
from jax.experimental.pallas import tpu as pltpu
from jax.sharding import Mesh, PartitionSpec as P

TD = 1408
TH = 16
EPSILON = 1e-06
DP = ("z", "x", "c")
BF = jnp.bfloat16
F32 = jnp.float32


def layer_norm(values, gain):
    mean_val = jnp.mean(values, axis=-1, keepdims=True)
    centred = values - mean_val
    spread = jnp.mean(centred * centred, axis=-1, keepdims=True)
    return centred * lax.rsqrt(spread + EPSILON) * gain


def shift(amount):
    return [(i, (i + amount) % 8) for i in range(8)]


def ring(block):
    held = [block] + [None] * 7
    right = left = block
    for step in range(1, 5):
        right = lax.ppermute(right, "mp", shift(1))
        held[step] = right
        if step < 4:
            left = lax.ppermute(left, "mp", shift(-1))
            held[8 - step] = left
    return held


def to_tiles(shard, per_piece):
    rows, cols = shard.shape
    tiles = shard.reshape(rows // 16, 16, cols // 128, 128).transpose(0, 2, 1, 3)
    tiles = tiles.reshape(-1, 16, 128)
    spare = 16 * per_piece - tiles.shape[0]
    tiles = jnp.concatenate([tiles, jnp.zeros((spare, 16, 128), tiles.dtype)])
    return tiles.reshape(16, per_piece, 16, 128)


VMEM = pl.BlockSpec(memory_space=pltpu.VMEM)
SMEM = pl.BlockSpec(memory_space=pltpu.SMEM)
LANES = (((1,), (1,)), ((), ()))


def kernel_call(body, outs, scratch=(), flops=0, scalars=0, arrays=0, moved=0, limit=8):
    return pl.pallas_call(
        body,
        out_shape=outs,
        in_specs=[SMEM] * scalars + [VMEM] * arrays,
        out_specs=[VMEM] * len(outs),
        scratch_shapes=scratch,
        compiler_params=pltpu.CompilerParams(vmem_limit_bytes=limit << 20),
        cost_estimate=pl.CostEstimate(flops=flops, bytes_accessed=moved, transcendentals=0),
    )


def project_body(block, gain, weights, made):
    values = block[:, :TD].astype(F32)
    normed = layer_norm(values, gain[...]).astype(BF)
    gap = jnp.zeros((128, 40), F32)
    for j in range(3):
        part = lax.dot_general(normed, weights[j], LANES, preferred_element_type=F32)
        part = jnp.concatenate([part[:, :88], gap, part[:, 88:], gap], axis=1)
        made[:, 256 * j : 256 * j + 256] = part.astype(BF)


def project(block, gain, weights):
    return kernel_call(
        project_body,
        [jax.ShapeDtypeStruct((128, 768), BF)],
        flops=2 * 128 * 528 * TD,
        arrays=3,
        moved=2_500_000,
    )(block, gain, weights)[0]


def middle_body(me_ref, *refs):
    held, made, (place, gain, widen, narrow) = refs[:8], refs[8:16], refs[16:20]
    normed_out, active_out, slope_out, joint, own_out, picked_out = refs[20:26]
    rows_by, queries, keys, values = refs[26:]
    def prepare():
        me = me_ref[0]
        mine = pl.ds(pl.multiple_of(me * 64, 64), 64)

        for s in range(8):
            owner = lax.rem(me + (8 - s), 8)
            for g in range(4):
                rows_by[owner, 128 * g : 128 * g + 128, :] = held[s][
                    :, TD + 128 * g : TD + 128 * g + 128
                ]
        for b in range(8):
            own_out[:, 128 * b : 128 * b + 128] = rows_by[b, mine, :]

        spots = lax.broadcasted_iota(jnp.int32, (64, 128), 1)
        own_place = place[mine, :]
        total = jnp.zeros((64, TD), F32)
        for s in range(8):
            chosen = jnp.where(spots + 128 * s == own_place, 1.0, 0.0).astype(BF)
            total += jnp.dot(chosen, held[s][:, :TD], preferred_element_type=F32)
        picked_out[...] = total.astype(BF)

        for s in range(8):
            queries[128 * s : 128 * s + 128, :] = made[s][:, :256]
            keys[128 * s : 128 * s + 128, :] = made[s][:, 256:512]
            values[128 * s : 128 * s + 128, :] = made[s][:, 512:]

    step = pl.program_id(0)
    pl.when(step == 0)(prepare)
    rows = pl.ds(pl.multiple_of(step * 128, 128), 128)
    student = jnp.concatenate([rows_by[b, rows, :] for b in range(8)], axis=1).astype(F32)
    normed = layer_norm(student, gain[...]).astype(BF)
    normed_out[...] = normed
    pre = jnp.dot(normed, widen[...], preferred_element_type=F32)
    half = 0.5 * (1.0 + lax.erf(pre * 0.7071067811865476))
    active = (pre * half).astype(BF)
    active_out[...] = active
    slope_out[...] = half + pre * 0.3989422804014327 * jnp.exp(-0.5 * pre * pre)
    joint[:, :1024] = jnp.dot(active, narrow[...], preferred_element_type=F32).astype(BF)

    spots = lax.broadcasted_iota(jnp.int32, (128, 1024), 1)
    chosen = jnp.where(spots == place[rows, :], 1.0, 0.0).astype(BF)
    query = jnp.dot(chosen, queries[...], preferred_element_type=F32).astype(BF)
    heads = []
    for h in range(2):
        lanes = slice(128 * h, 128 * h + 128)
        scores = lax.dot_general(
            query[:, lanes], keys[:, lanes], LANES, preferred_element_type=F32
        ) * ((TD // TH) ** (-0.5))
        top = jnp.max(scores, axis=-1, keepdims=True)
        num = jnp.exp(scores - top)
        soft = (num * (1.0 / jnp.sum(num, axis=-1, keepdims=True))).astype(BF)
        heads.append(jnp.dot(soft, values[:, lanes], preferred_element_type=F32)[:, :88])
    heads.append(jnp.zeros((128, 80), F32))
    joint[:, 1024:] = jnp.concatenate(heads, axis=1).astype(BF)


def middle(me, held, made, place, gain, widen, narrow):
    def banded(width):
        return pl.BlockSpec((128, width), lambda i: (i, 0))

    def once(width):
        return pl.BlockSpec((64, width), lambda i: (0, 0))

    return pl.pallas_call(
        middle_body,
        grid=(4,),
        out_shape=[
            jax.ShapeDtypeStruct((512, 1024), BF),
            jax.ShapeDtypeStruct((512, 512), BF),
            jax.ShapeDtypeStruct((512, 512), F32),
            jax.ShapeDtypeStruct((512, 1280), BF),
            jax.ShapeDtypeStruct((64, 1024), BF),
            jax.ShapeDtypeStruct((64, TD), BF),
        ],
        in_specs=[SMEM] + [VMEM] * 20,
        out_specs=[banded(1024), banded(512), banded(512), banded(1280), once(1024), once(TD)],
        scratch_shapes=[pltpu.VMEM((8, 512, 128), BF)] + [pltpu.VMEM((1024, 256), BF)] * 3,
        compiler_params=pltpu.CompilerParams(vmem_limit_bytes=14 << 20),
        cost_estimate=pl.CostEstimate(
            flops=2 * 512 * 1024 * (1024 + 768) + 2 * 64 * 1024 * TD,
            bytes_accessed=12_000_000,
            transcendentals=0,
        ),
    )(me, *held, *made, place, gain, widen, narrow)


def loss_body(weight, arrived, own, picked, out_full, head_full, back_out):
    branch = arrived[0, :, :1024].astype(F32)
    for b in range(1, 8):
        branch += arrived[b, :, :1024].astype(F32)
    outputs = (own[...].astype(F32) + branch).astype(BF)
    joined = jnp.concatenate([arrived[b, :, 1024:].astype(F32)[:, :176] for b in range(8)], axis=1).astype(BF)
    blended = lax.dot_general(joined, out_full[...], LANES, preferred_element_type=F32)
    targets = (picked[...].astype(F32) + blended).astype(BF).astype(F32)
    predicted = lax.dot_general(outputs, head_full[...], LANES, preferred_element_type=F32)
    inner = jnp.sum(predicted * targets, axis=-1, keepdims=True)
    inv_pred = lax.rsqrt(jnp.sum(predicted * predicted, axis=-1, keepdims=True) + EPSILON)
    inv_target = lax.rsqrt(jnp.sum(targets * targets, axis=-1, keepdims=True) + EPSILON)
    cosine = inner * inv_pred * inv_target
    row_weight = weight[...]
    slope = (row_weight * cosine * inv_pred * inv_pred) * predicted - (
        row_weight * inv_pred * inv_target
    ) * targets
    back = jnp.dot(slope.astype(BF), head_full[...], preferred_element_type=F32).astype(BF)
    loss = jnp.sum(row_weight * (1.0 - cosine), axis=0, keepdims=True)
    high = loss.astype(BF).astype(F32)
    lane = lax.broadcasted_iota(jnp.int32, (16, 128), 1)
    row = lax.broadcasted_iota(jnp.int32, (16, 128), 0)
    extra = jnp.where(lane == 0, high, jnp.where(lane == 1, loss - high, 0.0))
    extra = jnp.where(row == 0, extra, 0.0).astype(BF)
    for peer in range(8):
        for t in range(32):
            r, c = 16 * (t // 8), 128 * (t % 8)
            back_out[peer, t] = back[r : r + 16, c : c + 128]
        back_out[peer, 32] = extra


def loss_step(weight, arrived, own, picked, out_full, head_full):
    return kernel_call(
        loss_body,
        [jax.ShapeDtypeStruct((8, 33, 16, 128), BF)],
        flops=2 * 64 * 1408 * (1408 + 2048),
        arrays=6,
        moved=10_000_000,
    )(weight, arrived, own, picked, out_full, head_full)[0]


def assemble_body(pieces, out_full, head_full):
    def shard(y, _):
        for t in range(121):
            rows = pl.ds(pl.multiple_of(y * 176 + 16 * (t // 11), 16), 16)
            col = 128 * (t % 11)
            out_full[rows, col : col + 128] = pieces[t // 8, y, t % 8]
        for t in range(88):
            rows = pl.ds(pl.multiple_of(y * 176 + 16 * (t // 8), 16), 16)
            col = 128 * (t % 8)
            head_full[rows, col : col + 128] = pieces[t // 6, y, 8 + t % 6]
        return 0

    lax.fori_loop(0, 8, shard, 0)


def assemble(pieces):
    return kernel_call(
        assemble_body,
        [jax.ShapeDtypeStruct((TD, TD), BF), jax.ShapeDtypeStruct((TD, 1024), BF)],
        arrays=1,
        moved=14_000_000,
    )(pieces)


def tail_body(core_ref, back_in, normed, active, slope, narrow, keep, send, loss, back, pre):
    core = core_ref[0]
    for y in range(8):
        for t in range(32):
            r, c = 64 * y + 16 * (t // 8), 128 * (t % 8)
            back[r : r + 16, c : c + 128] = back_in[y, t]
    total = back_in[0, 32].astype(F32)
    for y in range(1, 8):
        total += back_in[y, 32].astype(F32)
    loss[0] = jnp.sum(total)

    def rows_chunk(i, _):
        rows = pl.ds(pl.multiple_of(i * 128, 128), 128)
        got = lax.dot_general(back[rows, :], narrow[...], LANES, preferred_element_type=F32)
        pre[rows, :] = (got * slope[rows, :]).astype(BF)
        return 0

    lax.fori_loop(0, 4, rows_chunk, 0)
    over_rows = (((0,), (0,)), ((), ()))

    def column_chunk(j, _):
        cols = pl.ds(pl.multiple_of(j * 128, 128), 128)
        grad_w = lax.dot_general(
            normed[:, cols], pre[...], over_rows, preferred_element_type=F32
        ).astype(BF)
        grad_n = lax.dot_general(
            back[:, cols], active[...], over_rows, preferred_element_type=F32
        ).astype(BF)

        def put(even, odd):
            for q in range(8):
                target = odd if q % 2 else even
                target[4 * j + q // 2, :16, :] = grad_w[16 * q : 16 * q + 16]
                target[4 * j + q // 2, 16:, :] = grad_n[16 * q : 16 * q + 16]

        pl.when(core == 0)(lambda: put(keep, send))
        pl.when(core == 1)(lambda: put(send, keep))
        return 0

    lax.fori_loop(0, 8, column_chunk, 0)


def tail(core, back, normed, active, slope, narrow):
    half = jax.ShapeDtypeStruct((32, 32, 512), BF)
    return pl.pallas_call(
        tail_body,
        out_shape=[half, half, jax.ShapeDtypeStruct((1,), F32)],
        in_specs=[SMEM] + [VMEM] * 5,
        out_specs=[VMEM, VMEM, SMEM],
        scratch_shapes=[pltpu.VMEM((512, 1024), BF), pltpu.VMEM((512, 512), BF)],
        compiler_params=pltpu.CompilerParams(vmem_limit_bytes=12 << 20),
        cost_estimate=pl.CostEstimate(
            flops=6 * 512 * 1024 * 512, bytes_accessed=8_000_000, transcendentals=0
        ),
    )(core, back, normed, active, slope, narrow)


def on_device(
    teacher_in,
    teacher_gain,
    teacher_qkv,
    teacher_out,
    student_in,
    student_gain,
    widen_weight,
    narrow_weight,
    target_head,
    positions,
    counts,
):
    me = lax.axis_index("mp")
    picked = positions[0]
    live_count = counts[0]

    rows = student_in[0][picked]
    packed = jnp.concatenate([rows[128 * g : 128 * g + 128] for g in range(4)], axis=1)
    held = ring(jnp.concatenate([teacher_in[0], packed], axis=1))

    at = lax.axis_index(("z", "c"))
    mine = jnp.concatenate(
        [
            lax.dynamic_index_in_dim(to_tiles(teacher_out, 8), at, 0, False),
            lax.dynamic_index_in_dim(to_tiles(target_head, 6), at, 0, False),
        ]
    )
    pieces = lax.all_gather(mine, ("z", "c", "mp"), axis=0)
    out_full, head_full = assemble(pieces.reshape(16, 8, 14, 16, 128))

    here = jnp.reshape(me, (1,)).astype(jnp.int32)
    made = [project(h, teacher_gain.reshape(1, -1), teacher_qkv) for h in held]
    place = ((me - picked // 128) % 8) * 128 + picked % 128
    normed_rows, activity, slope_pre, joint, own_rows, own_patches = middle(
        here,
        held,
        made,
        place.reshape(512, 1),
        student_gain.reshape(1, -1),
        widen_weight,
        narrow_weight,
    )
    arrived = lax.all_to_all(joint.reshape(8, 64, 1280), "mp", 0, 0, tiled=True)

    slot = me * 64 + jnp.arange(64, dtype=jnp.int32)
    row_weight = jnp.where(slot < live_count, 1.0 / live_count.astype(F32), jnp.zeros((), F32))
    back_own = loss_step(
        row_weight.reshape(64, 1), arrived, own_rows, own_patches, out_full, head_full
    )
    back = lax.all_to_all(back_own, "mp", 0, 0, tiled=True)

    core = jnp.reshape(lax.axis_index("c"), (1,)).astype(jnp.int32)
    keep, send, image_loss = tail(core, back, normed_rows, activity, slope_pre, narrow_weight)
    other = lax.ppermute(send, "c", [(0, 1), (1, 0)])
    kept = (keep.astype(F32) + other.astype(F32)).astype(BF)
    kept = lax.all_to_all(kept, ("z", "x"), 0, 0, tiled=True)
    total = jnp.sum(kept.astype(F32), axis=0)
    return (total[:16], total[16:], image_loss)


def solution(mesh):
    grid = Mesh(mesh.devices.reshape(8, 4, 2, 8), ("z", "x", "c", "mp"))
    placed = (
        P(DP, "mp", None),
        P(),
        P(None, "mp", None),
        P("mp", None),
        P(DP, None, "mp"),
        P(),
        P(None, "mp"),
        P("mp", None),
        P("mp", None),
        P(DP, None),
        P(DP),
    )
    return jax.shard_map(
        on_device,
        mesh=grid,
        in_specs=placed,
        out_specs=(P(DP, "mp"), P(DP, "mp"), P(DP)),
        check_vma=False,
    )
```

```python
import jax
import jax.numpy as jnp
from jax import lax
from jax.experimental import pallas as pl
from jax.experimental.pallas import tpu as pltpu
from jax.sharding import Mesh, PartitionSpec as P

TD = 1408
TH = 16
EPSILON = 1e-06
DP = ("z", "x", "c")
BF = jnp.bfloat16
F32 = jnp.float32


def layer_norm(values, gain):
    mean_val = jnp.mean(values, axis=-1, keepdims=True)
    centred = values - mean_val
    spread = jnp.mean(centred * centred, axis=-1, keepdims=True)
    return centred * lax.rsqrt(spread + EPSILON) * gain


def shift(amount):
    return [(i, (i + amount) % 8) for i in range(8)]


def ring(block):
    held = [block] + [None] * 7
    right = left = block
    for step in range(1, 5):
        right = lax.ppermute(right, "mp", shift(1))
        held[step] = right
        if step < 4:
            left = lax.ppermute(left, "mp", shift(-1))
            held[8 - step] = left
    return held


def to_tiles(shard):
    rows, cols = shard.shape
    tiles = shard.reshape(rows // 16, 16, cols // 128, 128).transpose(0, 2, 1, 3)
    tiles = tiles.reshape(-1, 16, 128)
    spare = 128 - tiles.shape[0]
    tiles = jnp.concatenate([tiles, jnp.zeros((spare, 16, 128), tiles.dtype)])
    return tiles.reshape(64, 2, 16, 128)


def to_everyone(array, axis, peers):
    copies = jnp.broadcast_to(array, (peers, *array.shape))
    return lax.all_to_all(copies, axis, 0, 0, tiled=True)


VMEM = pl.BlockSpec(memory_space=pltpu.VMEM)
HBM = pl.BlockSpec(memory_space=pltpu.HBM)
SMEM = pl.BlockSpec(memory_space=pltpu.SMEM)
LANES = (((1,), (1,)), ((), ()))


def kernel_call(body, outs, scratch=(), flops=0, scalars=0, arrays=0, moved=0, limit=8):
    return pl.pallas_call(
        body,
        out_shape=outs,
        in_specs=[SMEM] * scalars + [VMEM] * arrays,
        out_specs=[VMEM] * len(outs),
        scratch_shapes=scratch,
        compiler_params=pltpu.CompilerParams(vmem_limit_bytes=limit << 20),
        cost_estimate=pl.CostEstimate(flops=flops, bytes_accessed=moved, transcendentals=0),
    )


def project_body(block, gain, weights, made):
    values = block[:, :TD].astype(F32)
    normed = layer_norm(values, gain[...]).astype(BF)
    gap = jnp.zeros((128, 40), F32)
    for j in range(3):
        part = lax.dot_general(normed, weights[j], LANES, preferred_element_type=F32)
        part = jnp.concatenate([part[:, :88], gap, part[:, 88:], gap], axis=1)
        made[:, 256 * j : 256 * j + 256] = part.astype(BF)


def project(block, gain, weights):
    return kernel_call(
        project_body,
        [jax.ShapeDtypeStruct((128, 768), BF)],
        flops=2 * 128 * 528 * TD,
        arrays=3,
        moved=2_500_000,
    )(block, gain, weights)[0]


def middle_body(me_ref, *refs):
    held, made, (place, gain, widen, narrow) = refs[:8], refs[8:16], refs[16:20]
    *far, joint, own_out, picked_out = refs[20:26]
    rows_by, queries, keys, values, normed_out, active_out, slope_out, sent = refs[26:]

    def prepare():
        me = me_ref[0]
        mine = pl.ds(pl.multiple_of(me * 64, 64), 64)

        for s in range(8):
            owner = lax.rem(me + (8 - s), 8)
            for g in range(4):
                rows_by[owner, 128 * g : 128 * g + 128, :] = held[s][
                    :, TD + 128 * g : TD + 128 * g + 128
                ]
        for b in range(8):
            own_out[:, 128 * b : 128 * b + 128] = rows_by[b, mine, :]

        spots = lax.broadcasted_iota(jnp.int32, (64, 128), 1)
        own_place = place[mine, :]
        total = jnp.zeros((64, TD), F32)
        for s in range(8):
            chosen = jnp.where(spots + 128 * s == own_place, 1.0, 0.0).astype(BF)
            total += jnp.dot(chosen, held[s][:, :TD], preferred_element_type=F32)
        picked_out[...] = total.astype(BF)

        for s in range(8):
            queries[128 * s : 128 * s + 128, :] = made[s][:, :256]
            keys[128 * s : 128 * s + 128, :] = made[s][:, 256:512]
            values[128 * s : 128 * s + 128, :] = made[s][:, 512:]

    step = pl.program_id(0)
    pl.when(step == 0)(prepare)
    rows = pl.ds(pl.multiple_of(step * 128, 128), 128)
    student = jnp.concatenate([rows_by[b, rows, :] for b in range(8)], axis=1).astype(F32)
    normed = layer_norm(student, gain[...]).astype(BF)
    normed_out[rows, :] = normed
    pre = jnp.dot(normed, widen[...], preferred_element_type=F32)
    half = 0.5 * (1.0 + lax.erf(pre * 0.7071067811865476))
    active = (pre * half).astype(BF)
    active_out[rows, :] = active
    slope_out[rows, :] = half + pre * 0.3989422804014327 * jnp.exp(-0.5 * pre * pre)
    joint[:, :1024] = jnp.dot(active, narrow[...], preferred_element_type=F32).astype(BF)

    spots = lax.broadcasted_iota(jnp.int32, (128, 1024), 1)
    chosen = jnp.where(spots == place[rows, :], 1.0, 0.0).astype(BF)
    query = jnp.dot(chosen, queries[...], preferred_element_type=F32).astype(BF)
    heads = []
    for h in range(2):
        lanes = slice(128 * h, 128 * h + 128)
        scores = lax.dot_general(
            query[:, lanes], keys[:, lanes], LANES, preferred_element_type=F32
        ) * ((TD // TH) ** (-0.5))
        top = jnp.max(scores, axis=-1, keepdims=True)
        num = jnp.exp(scores - top)
        soft = (num * (1.0 / jnp.sum(num, axis=-1, keepdims=True))).astype(BF)
        heads.append(jnp.dot(soft, values[:, lanes], preferred_element_type=F32)[:, :88])
    heads.append(jnp.zeros((128, 80), F32))
    joint[:, 1024:] = jnp.concatenate(heads, axis=1).astype(BF)

    def sending(k, band):
        near = (normed_out, active_out, slope_out)[k]
        band_rows = pl.ds(pl.multiple_of(band * 128, 128), 128)
        return pltpu.make_async_copy(
            near.at[band_rows, :], far[k].at[band_rows, :], sent.at[k, band]
        )

    for k in range(3):
        sending(k, step).start()

    def finish():
        for k in range(3):
            for band in range(4):
                sending(k, band).wait()

    pl.when(step == 3)(finish)


def middle(me, held, made, place, gain, widen, narrow):
    def banded(width):
        return pl.BlockSpec((128, width), lambda i: (i, 0))

    def once(width):
        return pl.BlockSpec((64, width), lambda i: (0, 0))

    return pl.pallas_call(
        middle_body,
        grid=(4,),
        out_shape=[
            jax.ShapeDtypeStruct((512, 1024), BF),
            jax.ShapeDtypeStruct((512, 512), BF),
            jax.ShapeDtypeStruct((512, 512), F32),
            jax.ShapeDtypeStruct((512, 1280), BF),
            jax.ShapeDtypeStruct((64, 1024), BF),
            jax.ShapeDtypeStruct((64, TD), BF),
        ],
        in_specs=[SMEM] + [VMEM] * 20,
        out_specs=[HBM, HBM, HBM, banded(1280), once(1024), once(TD)],
        scratch_shapes=[pltpu.VMEM((8, 512, 128), BF)]
        + [pltpu.VMEM((1024, 256), BF)] * 3
        + [
            pltpu.VMEM((512, 1024), BF),
            pltpu.VMEM((512, 512), BF),
            pltpu.VMEM((512, 512), F32),
            pltpu.SemaphoreType.DMA((3, 4)),
        ],
        compiler_params=pltpu.CompilerParams(vmem_limit_bytes=48 << 20),
        cost_estimate=pl.CostEstimate(
            flops=2 * 512 * 1024 * (1024 + 768) + 2 * 64 * 1024 * TD,
            bytes_accessed=12_000_000,
            transcendentals=0,
        ),
    )(me, *held, *made, place, gain, widen, narrow)


def loss_body(
    weight, arrived, own, picked, out_far, head_far, back_out, out_full, head_full, arrivals
):
    out_copy = pltpu.make_async_copy(out_far, out_full, arrivals.at[0])
    head_copy = pltpu.make_async_copy(head_far, head_full, arrivals.at[1])
    out_copy.start()
    head_copy.start()
    branch = arrived[0, :, :1024].astype(F32)
    for b in range(1, 8):
        branch += arrived[b, :, :1024].astype(F32)
    outputs = (own[...].astype(F32) + branch).astype(BF)
    joined = jnp.concatenate([arrived[b, :, 1024:].astype(F32)[:, :176] for b in range(8)], axis=1).astype(BF)
    out_copy.wait()
    blended = lax.dot_general(joined, out_full[...], LANES, preferred_element_type=F32)
    targets = (picked[...].astype(F32) + blended).astype(BF).astype(F32)
    head_copy.wait()
    predicted = lax.dot_general(outputs, head_full[...], LANES, preferred_element_type=F32)
    inner = jnp.sum(predicted * targets, axis=-1, keepdims=True)
    inv_pred = lax.rsqrt(jnp.sum(predicted * predicted, axis=-1, keepdims=True) + EPSILON)
    inv_target = lax.rsqrt(jnp.sum(targets * targets, axis=-1, keepdims=True) + EPSILON)
    cosine = inner * inv_pred * inv_target
    row_weight = weight[...]
    slope = (row_weight * cosine * inv_pred * inv_pred) * predicted - (
        row_weight * inv_pred * inv_target
    ) * targets
    back = jnp.dot(slope.astype(BF), head_full[...], preferred_element_type=F32).astype(BF)
    loss = jnp.sum(row_weight * (1.0 - cosine), axis=0, keepdims=True)
    high = loss.astype(BF).astype(F32)
    lane = lax.broadcasted_iota(jnp.int32, (16, 128), 1)
    row = lax.broadcasted_iota(jnp.int32, (16, 128), 0)
    extra = jnp.where(lane == 0, high, jnp.where(lane == 1, loss - high, 0.0))
    extra = jnp.where(row == 0, extra, 0.0).astype(BF)
    for peer in range(8):
        for t in range(32):
            r, c = 16 * (t // 8), 128 * (t % 8)
            back_out[peer, t] = back[r : r + 16, c : c + 128]
        back_out[peer, 32] = extra


def loss_step(weight, arrived, own, picked, out_full, head_full):
    return pl.pallas_call(
        loss_body,
        out_shape=jax.ShapeDtypeStruct((8, 33, 16, 128), BF),
        in_specs=[VMEM] * 4 + [HBM] * 2,
        out_specs=VMEM,
        scratch_shapes=[
            pltpu.VMEM((TD, TD), BF),
            pltpu.VMEM((TD, 1024), BF),
            pltpu.SemaphoreType.DMA((2,)),
        ],
        compiler_params=pltpu.CompilerParams(vmem_limit_bytes=51 << 20),
        cost_estimate=pl.CostEstimate(
            flops=2 * 64 * 1408 * (1408 + 2048), bytes_accessed=10_000_000, transcendentals=0
        ),
    )(weight, arrived, own, picked, out_full, head_full)


def assemble_body(pieces, out_full, head_full):
    def shard(y, _):
        for t in range(121):
            rows = pl.ds(pl.multiple_of(y * 176 + 16 * (t // 11), 16), 16)
            col = 128 * (t % 11)
            out_full[rows, col : col + 128] = pieces[t // 8, t // 2 % 4, y, t % 2]
        for t in range(88):
            rows = pl.ds(pl.multiple_of(y * 176 + 16 * (t // 8), 16), 16)
            col = 128 * (t % 8)
            head_full[rows, col : col + 128] = pieces[t // 8, t // 2 % 4, y, 2 + t % 2]
        return 0

    lax.fori_loop(0, 8, shard, 0)


def assemble(pieces):
    return kernel_call(
        assemble_body,
        [jax.ShapeDtypeStruct((TD, TD), BF), jax.ShapeDtypeStruct((TD, 1024), BF)],
        arrays=1,
        moved=14_000_000,
    )(pieces)


def tail_body(core_ref, back_in, normed, active, slope, narrow, keep, send, loss, back, pre):
    core = core_ref[0]
    for y in range(8):
        for t in range(32):
            r, c = 64 * y + 16 * (t // 8), 128 * (t % 8)
            back[r : r + 16, c : c + 128] = back_in[y, t]
    total = back_in[0, 32].astype(F32)
    for y in range(1, 8):
        total += back_in[y, 32].astype(F32)
    loss[0] = jnp.sum(total)

    def rows_chunk(i, _):
        rows = pl.ds(pl.multiple_of(i * 128, 128), 128)
        got = lax.dot_general(back[rows, :], narrow[...], LANES, preferred_element_type=F32)
        pre[rows, :] = (got * slope[rows, :]).astype(BF)
        return 0

    lax.fori_loop(0, 4, rows_chunk, 0)
    over_rows = (((0,), (0,)), ((), ()))

    def column_chunk(j, _):
        cols = pl.ds(pl.multiple_of(j * 128, 128), 128)
        grad_w = lax.dot_general(
            normed[:, cols], pre[...], over_rows, preferred_element_type=F32
        ).astype(BF)
        grad_n = lax.dot_general(
            back[:, cols], active[...], over_rows, preferred_element_type=F32
        ).astype(BF)

        def put(even, odd):
            for q in range(8):
                target = odd if q % 2 else even
                target[4 * j + q // 2, :16, :] = grad_w[16 * q : 16 * q + 16]
                target[4 * j + q // 2, 16:, :] = grad_n[16 * q : 16 * q + 16]

        pl.when(core == 0)(lambda: put(keep, send))
        pl.when(core == 1)(lambda: put(send, keep))
        return 0

    lax.fori_loop(0, 8, column_chunk, 0)


def tail(core, back, normed, active, slope, narrow):
    half = jax.ShapeDtypeStruct((32, 32, 512), BF)
    return pl.pallas_call(
        tail_body,
        out_shape=[half, half, jax.ShapeDtypeStruct((1,), F32)],
        in_specs=[SMEM] + [VMEM] * 5,
        out_specs=[VMEM, VMEM, SMEM],
        scratch_shapes=[pltpu.VMEM((512, 1024), BF), pltpu.VMEM((512, 512), BF)],
        compiler_params=pltpu.CompilerParams(vmem_limit_bytes=12 << 20),
        cost_estimate=pl.CostEstimate(
            flops=6 * 512 * 1024 * 512, bytes_accessed=8_000_000, transcendentals=0
        ),
    )(core, back, normed, active, slope, narrow)


def on_device(
    teacher_in,
    teacher_gain,
    teacher_qkv,
    teacher_out,
    student_in,
    student_gain,
    widen_weight,
    narrow_weight,
    target_head,
    positions,
    counts,
):
    me = lax.axis_index("mp")
    picked = positions[0]
    live_count = counts[0]

    rows = student_in[0][picked]
    packed = jnp.concatenate([rows[128 * g : 128 * g + 128] for g in range(4)], axis=1)
    held = ring(jnp.concatenate([teacher_in[0], packed], axis=1))

    at = lax.axis_index(("z", "c", "x"))
    mine = jnp.concatenate(
        [
            lax.dynamic_index_in_dim(to_tiles(teacher_out), at, 0, False),
            lax.dynamic_index_in_dim(to_tiles(target_head), at, 0, False),
        ]
    )
    shares = to_everyone(to_everyone(mine, "mp", 8), "x", 4)
    shares, _, _ = lax.optimization_barrier((shares, held[1], held[7]))
    out_full, head_full = assemble(lax.all_gather(shares, ("z", "c"), axis=0))

    here = jnp.reshape(me, (1,)).astype(jnp.int32)
    made = [project(h, teacher_gain.reshape(1, -1), teacher_qkv) for h in held]
    place = ((me - picked // 128) % 8) * 128 + picked % 128
    normed_rows, activity, slope_pre, joint, own_rows, own_patches = middle(
        here,
        held,
        made,
        place.reshape(512, 1),
        student_gain.reshape(1, -1),
        widen_weight,
        narrow_weight,
    )
    arrived = lax.all_to_all(joint.reshape(8, 64, 1280), "mp", 0, 0, tiled=True)

    slot = me * 64 + jnp.arange(64, dtype=jnp.int32)
    row_weight = jnp.where(slot < live_count, 1.0 / live_count.astype(F32), jnp.zeros((), F32))
    back_own = loss_step(
        row_weight.reshape(64, 1), arrived, own_rows, own_patches, out_full, head_full
    )
    back = lax.all_to_all(back_own, "mp", 0, 0, tiled=True)

    core = jnp.reshape(lax.axis_index("c"), (1,)).astype(jnp.int32)
    keep, send, image_loss = tail(core, back, normed_rows, activity, slope_pre, narrow_weight)
    other = lax.ppermute(send, "c", [(0, 1), (1, 0)])
    kept = (keep.astype(F32) + other.astype(F32)).astype(BF)
    kept = lax.all_to_all(kept, ("z", "x"), 0, 0, tiled=True)
    total = jnp.sum(kept.astype(F32), axis=0)
    return (total[:16], total[16:], image_loss)


def solution(mesh):
    grid = Mesh(mesh.devices.reshape(8, 4, 2, 8), ("z", "x", "c", "mp"))
    placed = (
        P(DP, "mp", None),
        P(),
        P(None, "mp", None),
        P("mp", None),
        P(DP, None, "mp"),
        P(),
        P(None, "mp"),
        P("mp", None),
        P("mp", None),
        P(DP, None),
        P(DP),
    )
    return jax.shard_map(
        on_device,
        mesh=grid,
        in_specs=placed,
        out_specs=(P(DP, "mp"), P(DP, "mp"), P(DP)),
        check_vma=False,
    )
```

```python
import jax
import jax.numpy as jnp
from jax import lax
from jax.experimental import pallas as pl
from jax.experimental.pallas import tpu as pltpu
from jax.sharding import Mesh, PartitionSpec as P

TD = 1408
TH = 16
EPSILON = 1e-06
DP = ("z", "x", "c")
BF = jnp.bfloat16
F32 = jnp.float32


def layer_norm(values, gain):
    mean_val = jnp.mean(values, axis=-1, keepdims=True)
    centred = values - mean_val
    spread = jnp.mean(centred * centred, axis=-1, keepdims=True)
    return centred * lax.rsqrt(spread + EPSILON) * gain


def shift(amount):
    return [(i, (i + amount) % 8) for i in range(8)]


def ring(block):
    held = [block] + [None] * 7
    right = left = block
    for step in range(1, 5):
        right = lax.ppermute(right, "mp", shift(1))
        held[step] = right
        if step < 4:
            left = lax.ppermute(left, "mp", shift(-1))
            held[8 - step] = left
    return held


def to_tiles(shard, per_piece):
    rows, cols = shard.shape
    tiles = shard.reshape(rows // 16, 16, cols // 128, 128).transpose(0, 2, 1, 3)
    tiles = tiles.reshape(-1, 16, 128)
    spare = 16 * per_piece - tiles.shape[0]
    tiles = jnp.concatenate([tiles, jnp.zeros((spare, 16, 128), tiles.dtype)])
    return tiles.reshape(16, per_piece, 16, 128)


VMEM = pl.BlockSpec(memory_space=pltpu.VMEM)
HBM = pl.BlockSpec(memory_space=pltpu.HBM)
SMEM = pl.BlockSpec(memory_space=pltpu.SMEM)
LANES = (((1,), (1,)), ((), ()))


def kernel_call(body, outs, scratch=(), flops=0, scalars=0, arrays=0, moved=0, limit=8):
    return pl.pallas_call(
        body,
        out_shape=outs,
        in_specs=[SMEM] * scalars + [VMEM] * arrays,
        out_specs=[VMEM] * len(outs),
        scratch_shapes=scratch,
        compiler_params=pltpu.CompilerParams(vmem_limit_bytes=limit << 20),
        cost_estimate=pl.CostEstimate(flops=flops, bytes_accessed=moved, transcendentals=0),
    )


def project_body(block, gain, weights, made):
    values = block[:, :TD].astype(F32)
    normed = layer_norm(values, gain[...]).astype(BF)
    gap = jnp.zeros((128, 40), F32)
    for j in range(3):
        part = lax.dot_general(normed, weights[j], LANES, preferred_element_type=F32)
        part = jnp.concatenate([part[:, :88], gap, part[:, 88:], gap], axis=1)
        made[:, 256 * j : 256 * j + 256] = part.astype(BF)


def project(block, gain, weights):
    return kernel_call(
        project_body,
        [jax.ShapeDtypeStruct((128, 768), BF)],
        flops=2 * 128 * 528 * TD,
        arrays=3,
        moved=2_500_000,
    )(block, gain, weights)[0]


def middle_body(me_ref, *refs):
    held, made, (place, gain, widen, narrow) = refs[:8], refs[8:16], refs[16:20]
    *far, joint, own_out, picked_out = refs[20:26]
    rows_by, queries, keys, values, normed_out, active_out, slope_out, sent = refs[26:]

    def prepare():
        me = me_ref[0]
        mine = pl.ds(pl.multiple_of(me * 64, 64), 64)

        for s in range(8):
            owner = lax.rem(me + (8 - s), 8)
            for g in range(4):
                rows_by[owner, 128 * g : 128 * g + 128, :] = held[s][
                    :, TD + 128 * g : TD + 128 * g + 128
                ]
        for b in range(8):
            own_out[:, 128 * b : 128 * b + 128] = rows_by[b, mine, :]

        spots = lax.broadcasted_iota(jnp.int32, (64, 128), 1)
        own_place = place[mine, :]
        total = jnp.zeros((64, TD), F32)
        for s in range(8):
            chosen = jnp.where(spots + 128 * s == own_place, 1.0, 0.0).astype(BF)
            total += jnp.dot(chosen, held[s][:, :TD], preferred_element_type=F32)
        picked_out[...] = total.astype(BF)

        for s in range(8):
            queries[128 * s : 128 * s + 128, :] = made[s][:, :256]
            keys[128 * s : 128 * s + 128, :] = made[s][:, 256:512]
            values[128 * s : 128 * s + 128, :] = made[s][:, 512:]

    step = pl.program_id(0)
    pl.when(step == 0)(prepare)
    rows = pl.ds(pl.multiple_of(step * 128, 128), 128)
    student = jnp.concatenate([rows_by[b, rows, :] for b in range(8)], axis=1).astype(F32)
    normed = layer_norm(student, gain[...]).astype(BF)
    normed_out[rows, :] = normed
    pre = jnp.dot(normed, widen[...], preferred_element_type=F32)
    half = 0.5 * (1.0 + lax.erf(pre * 0.7071067811865476))
    active = (pre * half).astype(BF)
    active_out[rows, :] = active
    slope_out[rows, :] = half + pre * 0.3989422804014327 * jnp.exp(-0.5 * pre * pre)
    joint[:, :1024] = jnp.dot(active, narrow[...], preferred_element_type=F32).astype(BF)

    spots = lax.broadcasted_iota(jnp.int32, (128, 1024), 1)
    chosen = jnp.where(spots == place[rows, :], 1.0, 0.0).astype(BF)
    query = jnp.dot(chosen, queries[...], preferred_element_type=F32).astype(BF)
    heads = []
    for h in range(2):
        lanes = slice(128 * h, 128 * h + 128)
        scores = lax.dot_general(
            query[:, lanes], keys[:, lanes], LANES, preferred_element_type=F32
        ) * ((TD // TH) ** (-0.5))
        top = jnp.max(scores, axis=-1, keepdims=True)
        num = jnp.exp(scores - top)
        soft = (num * (1.0 / jnp.sum(num, axis=-1, keepdims=True))).astype(BF)
        heads.append(jnp.dot(soft, values[:, lanes], preferred_element_type=F32)[:, :88])
    heads.append(jnp.zeros((128, 80), F32))
    joint[:, 1024:] = jnp.concatenate(heads, axis=1).astype(BF)

    def sending(k, band):
        near = (normed_out, active_out, slope_out)[k]
        band_rows = pl.ds(pl.multiple_of(band * 128, 128), 128)
        return pltpu.make_async_copy(
            near.at[band_rows, :], far[k].at[band_rows, :], sent.at[k, band]
        )

    for k in range(3):
        sending(k, step).start()

    def finish():
        for k in range(3):
            for band in range(4):
                sending(k, band).wait()

    pl.when(step == 3)(finish)


def middle(me, held, made, place, gain, widen, narrow):
    def banded(width):
        return pl.BlockSpec((128, width), lambda i: (i, 0))

    def once(width):
        return pl.BlockSpec((64, width), lambda i: (0, 0))

    return pl.pallas_call(
        middle_body,
        grid=(4,),
        out_shape=[
            jax.ShapeDtypeStruct((512, 1024), BF),
            jax.ShapeDtypeStruct((512, 512), BF),
            jax.ShapeDtypeStruct((512, 512), F32),
            jax.ShapeDtypeStruct((512, 1280), BF),
            jax.ShapeDtypeStruct((64, 1024), BF),
            jax.ShapeDtypeStruct((64, TD), BF),
        ],
        in_specs=[SMEM] + [VMEM] * 20,
        out_specs=[HBM, HBM, HBM, banded(1280), once(1024), once(TD)],
        scratch_shapes=[pltpu.VMEM((8, 512, 128), BF)]
        + [pltpu.VMEM((1024, 256), BF)] * 3
        + [
            pltpu.VMEM((512, 1024), BF),
            pltpu.VMEM((512, 512), BF),
            pltpu.VMEM((512, 512), F32),
            pltpu.SemaphoreType.DMA((3, 4)),
        ],
        compiler_params=pltpu.CompilerParams(vmem_limit_bytes=48 << 20),
        cost_estimate=pl.CostEstimate(
            flops=2 * 512 * 1024 * (1024 + 768) + 2 * 64 * 1024 * TD,
            bytes_accessed=12_000_000,
            transcendentals=0,
        ),
    )(me, *held, *made, place, gain, widen, narrow)


def loss_body(
    weight, arrived, own, picked, out_far, head_far, back_out, out_full, head_full, arrivals
):
    out_copy = pltpu.make_async_copy(out_far, out_full, arrivals.at[0])
    head_copy = pltpu.make_async_copy(head_far, head_full, arrivals.at[1])
    out_copy.start()
    head_copy.start()
    branch = arrived[0, :, :1024].astype(F32)
    for b in range(1, 8):
        branch += arrived[b, :, :1024].astype(F32)
    outputs = (own[...].astype(F32) + branch).astype(BF)
    joined = jnp.concatenate([arrived[b, :, 1024:].astype(F32)[:, :176] for b in range(8)], axis=1).astype(BF)
    out_copy.wait()
    blended = lax.dot_general(joined, out_full[...], LANES, preferred_element_type=F32)
    targets = (picked[...].astype(F32) + blended).astype(BF).astype(F32)
    head_copy.wait()
    predicted = lax.dot_general(outputs, head_full[...], LANES, preferred_element_type=F32)
    inner = jnp.sum(predicted * targets, axis=-1, keepdims=True)
    inv_pred = lax.rsqrt(jnp.sum(predicted * predicted, axis=-1, keepdims=True) + EPSILON)
    inv_target = lax.rsqrt(jnp.sum(targets * targets, axis=-1, keepdims=True) + EPSILON)
    cosine = inner * inv_pred * inv_target
    row_weight = weight[...]
    slope = (row_weight * cosine * inv_pred * inv_pred) * predicted - (
        row_weight * inv_pred * inv_target
    ) * targets
    back = jnp.dot(slope.astype(BF), head_full[...], preferred_element_type=F32).astype(BF)
    loss = jnp.sum(row_weight * (1.0 - cosine), axis=0, keepdims=True)
    high = loss.astype(BF).astype(F32)
    lane = lax.broadcasted_iota(jnp.int32, (16, 128), 1)
    row = lax.broadcasted_iota(jnp.int32, (16, 128), 0)
    extra = jnp.where(lane == 0, high, jnp.where(lane == 1, loss - high, 0.0))
    extra = jnp.where(row == 0, extra, 0.0).astype(BF)
    for peer in range(8):
        for t in range(32):
            r, c = 16 * (t // 8), 128 * (t % 8)
            back_out[peer, t] = back[r : r + 16, c : c + 128]
        back_out[peer, 32] = extra


def loss_step(weight, arrived, own, picked, out_full, head_full):
    return pl.pallas_call(
        loss_body,
        out_shape=jax.ShapeDtypeStruct((8, 33, 16, 128), BF),
        in_specs=[VMEM] * 4 + [HBM] * 2,
        out_specs=VMEM,
        scratch_shapes=[
            pltpu.VMEM((TD, TD), BF),
            pltpu.VMEM((TD, 1024), BF),
            pltpu.SemaphoreType.DMA((2,)),
        ],
        compiler_params=pltpu.CompilerParams(vmem_limit_bytes=51 << 20),
        cost_estimate=pl.CostEstimate(
            flops=2 * 64 * 1408 * (1408 + 2048), bytes_accessed=10_000_000, transcendentals=0
        ),
    )(weight, arrived, own, picked, out_full, head_full)


def assemble_body(pieces, out_full, head_full):
    for t in range(121):
        r, c = 16 * (t // 11), 128 * (t % 11)
        out_full[r : r + 16, c : c + 128] = pieces[t // 8, 0, t % 8]
    for t in range(88):
        r, c = 16 * (t // 8), 128 * (t % 8)
        head_full[r : r + 16, c : c + 128] = pieces[t // 6, 0, 8 + t % 6]


def assemble(pieces):
    return pl.pallas_call(
        assemble_body,
        grid=(8,),
        out_shape=[jax.ShapeDtypeStruct((TD, TD), BF), jax.ShapeDtypeStruct((TD, 1024), BF)],
        in_specs=[pl.BlockSpec((16, 1, 14, 16, 128), lambda y: (0, y, 0, 0, 0))],
        out_specs=[
            pl.BlockSpec((176, TD), lambda y: (y, 0)),
            pl.BlockSpec((176, 1024), lambda y: (y, 0)),
        ],
        compiler_params=pltpu.CompilerParams(vmem_limit_bytes=56 << 20),
        cost_estimate=pl.CostEstimate(flops=0, bytes_accessed=14_000_000, transcendentals=0),
    )(pieces)


def tail_body(core_ref, back_in, normed, active, slope, narrow, keep, send, loss, back, pre):
    core = core_ref[0]
    for y in range(8):
        for t in range(32):
            r, c = 64 * y + 16 * (t // 8), 128 * (t % 8)
            back[r : r + 16, c : c + 128] = back_in[y, t]
    total = back_in[0, 32].astype(F32)
    for y in range(1, 8):
        total += back_in[y, 32].astype(F32)
    loss[0] = jnp.sum(total)

    def rows_chunk(i, _):
        rows = pl.ds(pl.multiple_of(i * 128, 128), 128)
        got = lax.dot_general(back[rows, :], narrow[...], LANES, preferred_element_type=F32)
        pre[rows, :] = (got * slope[rows, :]).astype(BF)
        return 0

    lax.fori_loop(0, 4, rows_chunk, 0)
    over_rows = (((0,), (0,)), ((), ()))

    def column_chunk(j, _):
        cols = pl.ds(pl.multiple_of(j * 128, 128), 128)
        grad_w = lax.dot_general(
            normed[:, cols], pre[...], over_rows, preferred_element_type=F32
        ).astype(BF)
        grad_n = lax.dot_general(
            back[:, cols], active[...], over_rows, preferred_element_type=F32
        ).astype(BF)

        def put(even, odd):
            for q in range(8):
                target = odd if q % 2 else even
                target[4 * j + q // 2, :16, :] = grad_w[16 * q : 16 * q + 16]
                target[4 * j + q // 2, 16:, :] = grad_n[16 * q : 16 * q + 16]

        pl.when(core == 0)(lambda: put(keep, send))
        pl.when(core == 1)(lambda: put(send, keep))
        return 0

    lax.fori_loop(0, 8, column_chunk, 0)


def tail(core, back, normed, active, slope, narrow):
    half = jax.ShapeDtypeStruct((32, 32, 512), BF)
    return pl.pallas_call(
        tail_body,
        out_shape=[half, half, jax.ShapeDtypeStruct((1,), F32)],
        in_specs=[SMEM] + [VMEM] * 5,
        out_specs=[VMEM, VMEM, SMEM],
        scratch_shapes=[pltpu.VMEM((512, 1024), BF), pltpu.VMEM((512, 512), BF)],
        compiler_params=pltpu.CompilerParams(vmem_limit_bytes=12 << 20),
        cost_estimate=pl.CostEstimate(
            flops=6 * 512 * 1024 * 512, bytes_accessed=8_000_000, transcendentals=0
        ),
    )(core, back, normed, active, slope, narrow)


def on_device(
    teacher_in,
    teacher_gain,
    teacher_qkv,
    teacher_out,
    student_in,
    student_gain,
    widen_weight,
    narrow_weight,
    target_head,
    positions,
    counts,
):
    me = lax.axis_index("mp")
    picked = positions[0]
    live_count = counts[0]

    rows = student_in[0][picked]
    packed = jnp.concatenate([rows[128 * g : 128 * g + 128] for g in range(4)], axis=1)
    held = ring(jnp.concatenate([teacher_in[0], packed], axis=1))

    at = lax.axis_index(("z", "c"))
    mine = jnp.concatenate(
        [
            lax.dynamic_index_in_dim(to_tiles(teacher_out, 8), at, 0, False),
            lax.dynamic_index_in_dim(to_tiles(target_head, 6), at, 0, False),
        ]
    )
    pieces = lax.all_gather(mine, ("z", "c", "mp"), axis=0)
    out_full, head_full = assemble(pieces.reshape(16, 8, 14, 16, 128))

    here = jnp.reshape(me, (1,)).astype(jnp.int32)
    made = [project(h, teacher_gain.reshape(1, -1), teacher_qkv) for h in held]
    place = ((me - picked // 128) % 8) * 128 + picked % 128
    normed_rows, activity, slope_pre, joint, own_rows, own_patches = middle(
        here,
        held,
        made,
        place.reshape(512, 1),
        student_gain.reshape(1, -1),
        widen_weight,
        narrow_weight,
    )
    arrived = lax.all_to_all(joint.reshape(8, 64, 1280), "mp", 0, 0, tiled=True)

    slot = me * 64 + jnp.arange(64, dtype=jnp.int32)
    row_weight = jnp.where(slot < live_count, 1.0 / live_count.astype(F32), jnp.zeros((), F32))
    back_own = loss_step(
        row_weight.reshape(64, 1), arrived, own_rows, own_patches, out_full, head_full
    )
    back = lax.all_to_all(back_own, "mp", 0, 0, tiled=True)

    core = jnp.reshape(lax.axis_index("c"), (1,)).astype(jnp.int32)
    keep, send, image_loss = tail(core, back, normed_rows, activity, slope_pre, narrow_weight)
    other = lax.ppermute(send, "c", [(0, 1), (1, 0)])
    kept = (keep.astype(F32) + other.astype(F32)).astype(BF)
    kept = lax.all_to_all(kept, ("z", "x"), 0, 0, tiled=True)
    total = jnp.sum(kept.astype(F32), axis=0)
    return (total[:16], total[16:], image_loss)


def solution(mesh):
    grid = Mesh(mesh.devices.reshape(8, 4, 2, 8), ("z", "x", "c", "mp"))
    placed = (
        P(DP, "mp", None),
        P(),
        P(None, "mp", None),
        P("mp", None),
        P(DP, None, "mp"),
        P(),
        P(None, "mp"),
        P("mp", None),
        P("mp", None),
        P(DP, None),
        P(DP),
    )
    return jax.shard_map(
        on_device,
        mesh=grid,
        in_specs=placed,
        out_specs=(P(DP, "mp"), P(DP, "mp"), P(DP)),
        check_vma=False,
    )
```

```python
import jax
import jax.numpy as jnp
from jax import lax
from jax.experimental import pallas as pl
from jax.experimental.pallas import tpu as pltpu
from jax.sharding import Mesh, PartitionSpec as P

TD = 1408
TH = 16
EPSILON = 1e-06
DP = ("z", "x", "c")
BF = jnp.bfloat16
F32 = jnp.float32


def layer_norm(values, gain):
    mean_val = jnp.mean(values, axis=-1, keepdims=True)
    centred = values - mean_val
    spread = jnp.mean(centred * centred, axis=-1, keepdims=True)
    return centred * lax.rsqrt(spread + EPSILON) * gain


def shift(amount):
    return [(i, (i + amount) % 8) for i in range(8)]


def ring(block):
    held = [block] + [None] * 7
    right = left = block
    for step in range(1, 5):
        right = lax.ppermute(right, "mp", shift(1))
        held[step] = right
        if step < 4:
            left = lax.ppermute(left, "mp", shift(-1))
            held[8 - step] = left
    return held


def to_tiles(shard):
    rows, cols = shard.shape
    tiles = shard.reshape(rows // 16, 16, cols // 128, 128).transpose(0, 2, 1, 3)
    tiles = tiles.reshape(-1, 16, 128)
    spare = 128 - tiles.shape[0]
    tiles = jnp.concatenate([tiles, jnp.zeros((spare, 16, 128), tiles.dtype)])
    return tiles.reshape(64, 2, 16, 128)


def to_everyone(array, axis, peers):
    copies = jnp.broadcast_to(array, (peers, *array.shape))
    return lax.all_to_all(copies, axis, 0, 0, tiled=True)


VMEM = pl.BlockSpec(memory_space=pltpu.VMEM)
HBM = pl.BlockSpec(memory_space=pltpu.HBM)
SMEM = pl.BlockSpec(memory_space=pltpu.SMEM)
LANES = (((1,), (1,)), ((), ()))


def kernel_call(body, outs, scratch=(), flops=0, scalars=0, arrays=0, moved=0, limit=8):
    return pl.pallas_call(
        body,
        out_shape=outs,
        in_specs=[SMEM] * scalars + [VMEM] * arrays,
        out_specs=[VMEM] * len(outs),
        scratch_shapes=scratch,
        compiler_params=pltpu.CompilerParams(vmem_limit_bytes=limit << 20),
        cost_estimate=pl.CostEstimate(flops=flops, bytes_accessed=moved, transcendentals=0),
    )


def project_body(block, gain, weights, made):
    values = block[:, :TD].astype(F32)
    normed = layer_norm(values, gain[...]).astype(BF)
    gap = jnp.zeros((128, 40), F32)
    for j in range(3):
        part = lax.dot_general(normed, weights[j], LANES, preferred_element_type=F32)
        part = jnp.concatenate([part[:, :88], gap, part[:, 88:], gap], axis=1)
        made[:, 256 * j : 256 * j + 256] = part.astype(BF)


def project(block, gain, weights):
    return kernel_call(
        project_body,
        [jax.ShapeDtypeStruct((128, 768), BF)],
        flops=2 * 128 * 528 * TD,
        arrays=3,
        moved=2_500_000,
    )(block, gain, weights)[0]


def middle_body(me_ref, *refs):
    held, made, (place, gain, widen, narrow) = refs[:8], refs[8:16], refs[16:20]
    *far, joint, own_out, picked_out = refs[20:26]
    rows_by, queries, keys, values, normed_out, active_out, slope_out, sent = refs[26:]

    def prepare():
        me = me_ref[0]
        mine = pl.ds(pl.multiple_of(me * 64, 64), 64)

        for s in range(8):
            owner = lax.rem(me + (8 - s), 8)
            for g in range(4):
                rows_by[owner, 128 * g : 128 * g + 128, :] = held[s][
                    :, TD + 128 * g : TD + 128 * g + 128
                ]
        for b in range(8):
            own_out[:, 128 * b : 128 * b + 128] = rows_by[b, mine, :]

        spots = lax.broadcasted_iota(jnp.int32, (64, 128), 1)
        own_place = place[mine, :]
        total = jnp.zeros((64, TD), F32)
        for s in range(8):
            chosen = jnp.where(spots + 128 * s == own_place, 1.0, 0.0).astype(BF)
            total += jnp.dot(chosen, held[s][:, :TD], preferred_element_type=F32)
        picked_out[...] = total.astype(BF)

        for s in range(8):
            queries[128 * s : 128 * s + 128, :] = made[s][:, :256]
            keys[128 * s : 128 * s + 128, :] = made[s][:, 256:512]
            values[128 * s : 128 * s + 128, :] = made[s][:, 512:]

    step = pl.program_id(0)
    pl.when(step == 0)(prepare)
    rows = pl.ds(pl.multiple_of(step * 128, 128), 128)
    student = jnp.concatenate([rows_by[b, rows, :] for b in range(8)], axis=1).astype(F32)
    normed = layer_norm(student, gain[...]).astype(BF)
    normed_out[rows, :] = normed
    pre = jnp.dot(normed, widen[...], preferred_element_type=F32)
    half = 0.5 * (1.0 + lax.erf(pre * 0.7071067811865476))
    active = (pre * half).astype(BF)
    active_out[rows, :] = active
    slope_out[rows, :] = half + pre * 0.3989422804014327 * jnp.exp(-0.5 * pre * pre)
    joint[:, :1024] = jnp.dot(active, narrow[...], preferred_element_type=F32).astype(BF)

    spots = lax.broadcasted_iota(jnp.int32, (128, 1024), 1)
    chosen = jnp.where(spots == place[rows, :], 1.0, 0.0).astype(BF)
    query = jnp.dot(chosen, queries[...], preferred_element_type=F32).astype(BF)
    heads = []
    for h in range(2):
        lanes = slice(128 * h, 128 * h + 128)
        scores = lax.dot_general(
            query[:, lanes], keys[:, lanes], LANES, preferred_element_type=F32
        ) * ((TD // TH) ** (-0.5))
        top = jnp.max(scores, axis=-1, keepdims=True)
        num = jnp.exp(scores - top)
        soft = (num * (1.0 / jnp.sum(num, axis=-1, keepdims=True))).astype(BF)
        heads.append(jnp.dot(soft, values[:, lanes], preferred_element_type=F32)[:, :88])
    heads.append(jnp.zeros((128, 80), F32))
    joint[:, 1024:] = jnp.concatenate(heads, axis=1).astype(BF)

    def sending(k, band):
        near = (normed_out, active_out, slope_out)[k]
        band_rows = pl.ds(pl.multiple_of(band * 128, 128), 128)
        return pltpu.make_async_copy(
            near.at[band_rows, :], far[k].at[band_rows, :], sent.at[k, band]
        )

    for k in range(3):
        sending(k, step).start()

    def finish():
        for k in range(3):
            for band in range(4):
                sending(k, band).wait()

    pl.when(step == 3)(finish)


def middle(me, held, made, place, gain, widen, narrow):
    def banded(width):
        return pl.BlockSpec((128, width), lambda i: (i, 0))

    def once(width):
        return pl.BlockSpec((64, width), lambda i: (0, 0))

    return pl.pallas_call(
        middle_body,
        grid=(4,),
        out_shape=[
            jax.ShapeDtypeStruct((512, 1024), BF),
            jax.ShapeDtypeStruct((512, 512), BF),
            jax.ShapeDtypeStruct((512, 512), F32),
            jax.ShapeDtypeStruct((512, 1280), BF),
            jax.ShapeDtypeStruct((64, 1024), BF),
            jax.ShapeDtypeStruct((64, TD), BF),
        ],
        in_specs=[SMEM] + [VMEM] * 20,
        out_specs=[HBM, HBM, HBM, banded(1280), once(1024), once(TD)],
        scratch_shapes=[pltpu.VMEM((8, 512, 128), BF)]
        + [pltpu.VMEM((1024, 256), BF)] * 3
        + [
            pltpu.VMEM((512, 1024), BF),
            pltpu.VMEM((512, 512), BF),
            pltpu.VMEM((512, 512), F32),
            pltpu.SemaphoreType.DMA((3, 4)),
        ],
        compiler_params=pltpu.CompilerParams(vmem_limit_bytes=48 << 20),
        cost_estimate=pl.CostEstimate(
            flops=2 * 512 * 1024 * (1024 + 768) + 2 * 64 * 1024 * TD,
            bytes_accessed=12_000_000,
            transcendentals=0,
        ),
    )(me, *held, *made, place, gain, widen, narrow)


def loss_body(
    weight, arrived, own, picked, out_far, head_far, back_out, out_full, head_full, arrivals
):
    out_copy = pltpu.make_async_copy(out_far, out_full, arrivals.at[0])
    head_copy = pltpu.make_async_copy(head_far, head_full, arrivals.at[1])
    out_copy.start()
    head_copy.start()
    branch = arrived[0, :, :1024].astype(F32)
    for b in range(1, 8):
        branch += arrived[b, :, :1024].astype(F32)
    outputs = (own[...].astype(F32) + branch).astype(BF)
    joined = jnp.concatenate([arrived[b, :, 1024:].astype(F32)[:, :176] for b in range(8)], axis=1).astype(BF)
    out_copy.wait()
    blended = lax.dot_general(joined, out_full[...], LANES, preferred_element_type=F32)
    targets = (picked[...].astype(F32) + blended).astype(BF).astype(F32)
    head_copy.wait()
    predicted = lax.dot_general(outputs, head_full[...], LANES, preferred_element_type=F32)
    inner = jnp.sum(predicted * targets, axis=-1, keepdims=True)
    inv_pred = lax.rsqrt(jnp.sum(predicted * predicted, axis=-1, keepdims=True) + EPSILON)
    inv_target = lax.rsqrt(jnp.sum(targets * targets, axis=-1, keepdims=True) + EPSILON)
    cosine = inner * inv_pred * inv_target
    row_weight = weight[...]
    slope = (row_weight * cosine * inv_pred * inv_pred) * predicted - (
        row_weight * inv_pred * inv_target
    ) * targets
    back = jnp.dot(slope.astype(BF), head_full[...], preferred_element_type=F32).astype(BF)
    loss = jnp.sum(row_weight * (1.0 - cosine), axis=0, keepdims=True)
    high = loss.astype(BF).astype(F32)
    lane = lax.broadcasted_iota(jnp.int32, (16, 128), 1)
    row = lax.broadcasted_iota(jnp.int32, (16, 128), 0)
    extra = jnp.where(lane == 0, high, jnp.where(lane == 1, loss - high, 0.0))
    extra = jnp.where(row == 0, extra, 0.0).astype(BF)
    for peer in range(8):
        for t in range(32):
            r, c = 16 * (t // 8), 128 * (t % 8)
            back_out[peer, t] = back[r : r + 16, c : c + 128]
        back_out[peer, 32] = extra


def loss_step(weight, arrived, own, picked, out_full, head_full):
    return pl.pallas_call(
        loss_body,
        out_shape=jax.ShapeDtypeStruct((8, 33, 16, 128), BF),
        in_specs=[VMEM] * 4 + [HBM] * 2,
        out_specs=VMEM,
        scratch_shapes=[
            pltpu.VMEM((TD, TD), BF),
            pltpu.VMEM((TD, 1024), BF),
            pltpu.SemaphoreType.DMA((2,)),
        ],
        compiler_params=pltpu.CompilerParams(vmem_limit_bytes=51 << 20),
        cost_estimate=pl.CostEstimate(
            flops=2 * 64 * 1408 * (1408 + 2048), bytes_accessed=10_000_000, transcendentals=0
        ),
    )(weight, arrived, own, picked, out_full, head_full)


def assemble_body(pieces, out_full, head_full):
    for t in range(121):
        r, c = 16 * (t // 11), 128 * (t % 11)
        out_full[r : r + 16, c : c + 128] = pieces[t // 8, t // 2 % 4, 0, t % 2]
    for t in range(88):
        r, c = 16 * (t // 8), 128 * (t % 8)
        head_full[r : r + 16, c : c + 128] = pieces[t // 8, t // 2 % 4, 0, 2 + t % 2]


def assemble(pieces):
    return pl.pallas_call(
        assemble_body,
        grid=(8,),
        out_shape=[jax.ShapeDtypeStruct((TD, TD), BF), jax.ShapeDtypeStruct((TD, 1024), BF)],
        in_specs=[pl.BlockSpec((16, 4, 1, 4, 16, 128), lambda y: (0, 0, y, 0, 0, 0))],
        out_specs=[
            pl.BlockSpec((176, TD), lambda y: (y, 0)),
            pl.BlockSpec((176, 1024), lambda y: (y, 0)),
        ],
        compiler_params=pltpu.CompilerParams(vmem_limit_bytes=56 << 20),
        cost_estimate=pl.CostEstimate(flops=0, bytes_accessed=14_000_000, transcendentals=0),
    )(pieces)


def tail_body(core_ref, back_in, normed, active, slope, narrow, keep, send, loss, back, pre):
    core = core_ref[0]
    for y in range(8):
        for t in range(32):
            r, c = 64 * y + 16 * (t // 8), 128 * (t % 8)
            back[r : r + 16, c : c + 128] = back_in[y, t]
    total = back_in[0, 32].astype(F32)
    for y in range(1, 8):
        total += back_in[y, 32].astype(F32)
    loss[0] = jnp.sum(total)

    def rows_chunk(i, _):
        rows = pl.ds(pl.multiple_of(i * 128, 128), 128)
        got = lax.dot_general(back[rows, :], narrow[...], LANES, preferred_element_type=F32)
        pre[rows, :] = (got * slope[rows, :]).astype(BF)
        return 0

    lax.fori_loop(0, 4, rows_chunk, 0)
    over_rows = (((0,), (0,)), ((), ()))

    def column_chunk(j, _):
        cols = pl.ds(pl.multiple_of(j * 128, 128), 128)
        grad_w = lax.dot_general(
            normed[:, cols], pre[...], over_rows, preferred_element_type=F32
        ).astype(BF)
        grad_n = lax.dot_general(
            back[:, cols], active[...], over_rows, preferred_element_type=F32
        ).astype(BF)

        def put(even, odd):
            for q in range(8):
                target = odd if q % 2 else even
                target[4 * j + q // 2, :16, :] = grad_w[16 * q : 16 * q + 16]
                target[4 * j + q // 2, 16:, :] = grad_n[16 * q : 16 * q + 16]

        pl.when(core == 0)(lambda: put(keep, send))
        pl.when(core == 1)(lambda: put(send, keep))
        return 0

    lax.fori_loop(0, 8, column_chunk, 0)


def tail(core, back, normed, active, slope, narrow):
    half = jax.ShapeDtypeStruct((32, 32, 512), BF)
    return pl.pallas_call(
        tail_body,
        out_shape=[half, half, jax.ShapeDtypeStruct((1,), F32)],
        in_specs=[SMEM] + [VMEM] * 5,
        out_specs=[VMEM, VMEM, SMEM],
        scratch_shapes=[pltpu.VMEM((512, 1024), BF), pltpu.VMEM((512, 512), BF)],
        compiler_params=pltpu.CompilerParams(vmem_limit_bytes=12 << 20),
        cost_estimate=pl.CostEstimate(
            flops=6 * 512 * 1024 * 512, bytes_accessed=8_000_000, transcendentals=0
        ),
    )(core, back, normed, active, slope, narrow)


def on_device(
    teacher_in,
    teacher_gain,
    teacher_qkv,
    teacher_out,
    student_in,
    student_gain,
    widen_weight,
    narrow_weight,
    target_head,
    positions,
    counts,
):
    me = lax.axis_index("mp")
    picked = positions[0]
    live_count = counts[0]

    rows = student_in[0][picked]
    packed = jnp.concatenate([rows[128 * g : 128 * g + 128] for g in range(4)], axis=1)
    held = ring(jnp.concatenate([teacher_in[0], packed], axis=1))

    at = lax.axis_index(("z", "c", "x"))
    mine = jnp.concatenate(
        [
            lax.dynamic_index_in_dim(to_tiles(teacher_out), at, 0, False),
            lax.dynamic_index_in_dim(to_tiles(target_head), at, 0, False),
        ]
    )
    shares = to_everyone(to_everyone(mine, "mp", 8), "x", 4)
    shares, _, _ = lax.optimization_barrier((shares, held[2], held[6]))
    out_full, head_full = assemble(lax.all_gather(shares, ("z", "c"), axis=0))

    here = jnp.reshape(me, (1,)).astype(jnp.int32)
    made = [project(h, teacher_gain.reshape(1, -1), teacher_qkv) for h in held]
    place = ((me - picked // 128) % 8) * 128 + picked % 128
    normed_rows, activity, slope_pre, joint, own_rows, own_patches = middle(
        here,
        held,
        made,
        place.reshape(512, 1),
        student_gain.reshape(1, -1),
        widen_weight,
        narrow_weight,
    )
    arrived = lax.all_to_all(joint.reshape(8, 64, 1280), "mp", 0, 0, tiled=True)

    slot = me * 64 + jnp.arange(64, dtype=jnp.int32)
    row_weight = jnp.where(slot < live_count, 1.0 / live_count.astype(F32), jnp.zeros((), F32))
    back_own = loss_step(
        row_weight.reshape(64, 1), arrived, own_rows, own_patches, out_full, head_full
    )
    back = lax.all_to_all(back_own, "mp", 0, 0, tiled=True)

    core = jnp.reshape(lax.axis_index("c"), (1,)).astype(jnp.int32)
    keep, send, image_loss = tail(core, back, normed_rows, activity, slope_pre, narrow_weight)
    other = lax.ppermute(send, "c", [(0, 1), (1, 0)])
    kept = (keep.astype(F32) + other.astype(F32)).astype(BF)
    kept = lax.all_to_all(kept, ("z", "x"), 0, 0, tiled=True)
    total = jnp.sum(kept.astype(F32), axis=0)
    return (total[:16], total[16:], image_loss)


def solution(mesh):
    grid = Mesh(mesh.devices.reshape(8, 4, 2, 8), ("z", "x", "c", "mp"))
    placed = (
        P(DP, "mp", None),
        P(),
        P(None, "mp", None),
        P("mp", None),
        P(DP, None, "mp"),
        P(),
        P(None, "mp"),
        P("mp", None),
        P("mp", None),
        P(DP, None),
        P(DP),
    )
    return jax.shard_map(
        on_device,
        mesh=grid,
        in_specs=placed,
        out_specs=(P(DP, "mp"), P(DP, "mp"), P(DP)),
        check_vma=False,
    )
```

```python
import jax
import jax.numpy as jnp
from jax import lax
from jax.experimental import pallas as pl
from jax.experimental.pallas import tpu as pltpu
from jax.sharding import Mesh, PartitionSpec as P

TD = 1408
TH = 16
EPSILON = 1e-06
DP = ("z", "x", "c")
BF = jnp.bfloat16
F32 = jnp.float32


def layer_norm(values, gain):
    mean_val = jnp.mean(values, axis=-1, keepdims=True)
    centred = values - mean_val
    spread = jnp.mean(centred * centred, axis=-1, keepdims=True)
    return centred * lax.rsqrt(spread + EPSILON) * gain


def shift(amount):
    return [(i, (i + amount) % 8) for i in range(8)]


def ring(block):
    held = [block] + [None] * 7
    right = left = block
    for step in range(1, 5):
        right = lax.ppermute(right, "mp", shift(1))
        held[step] = right
        if step < 4:
            left = lax.ppermute(left, "mp", shift(-1))
            held[8 - step] = left
    return held


def to_tiles(shard, per_piece):
    rows, cols = shard.shape
    tiles = shard.reshape(rows // 16, 16, cols // 128, 128).transpose(0, 2, 1, 3)
    tiles = tiles.reshape(-1, 16, 128)
    spare = 16 * per_piece - tiles.shape[0]
    tiles = jnp.concatenate([tiles, jnp.zeros((spare, 16, 128), tiles.dtype)])
    return tiles.reshape(16, per_piece, 16, 128)


VMEM = pl.BlockSpec(memory_space=pltpu.VMEM)
HBM = pl.BlockSpec(memory_space=pltpu.HBM)
SMEM = pl.BlockSpec(memory_space=pltpu.SMEM)
LANES = (((1,), (1,)), ((), ()))


def kernel_call(body, outs, scratch=(), flops=0, scalars=0, arrays=0, moved=0, limit=8):
    return pl.pallas_call(
        body,
        out_shape=outs,
        in_specs=[SMEM] * scalars + [VMEM] * arrays,
        out_specs=[VMEM] * len(outs),
        scratch_shapes=scratch,
        compiler_params=pltpu.CompilerParams(vmem_limit_bytes=limit << 20),
        cost_estimate=pl.CostEstimate(flops=flops, bytes_accessed=moved, transcendentals=0),
    )


def project_body(block, gain, weights, place, before, made, after):
    values = block[:, :TD].astype(F32)
    normed = layer_norm(values, gain[...]).astype(BF)
    gap = jnp.zeros((128, 40), F32)
    for j in range(3):
        part = lax.dot_general(normed, weights[j], LANES, preferred_element_type=F32)
        part = jnp.concatenate([part[:, :88], gap, part[:, 88:], gap], axis=1)
        made[:, 256 * j : 256 * j + 256] = part.astype(BF)
    spots = lax.broadcasted_iota(jnp.int32, (64, 128), 1)
    chosen = jnp.where(spots == place[...], 1.0, 0.0).astype(BF)
    own = jnp.dot(chosen, block[:, :TD], preferred_element_type=F32)
    after[...] = (before[...].astype(F32) + own).astype(BF)


def project(block, gain, weights, place, before):
    return kernel_call(
        project_body,
        [jax.ShapeDtypeStruct((128, 768), BF), jax.ShapeDtypeStruct((64, TD), BF)],
        flops=2 * 128 * (528 + 64) * TD,
        arrays=5,
        moved=2_500_000,
    )(block, gain, weights, place, before)


def middle_body(me_ref, *refs):
    held, made, (place, gain, widen, narrow) = refs[:8], refs[8:16], refs[16:20]
    *far, joint, own_out = refs[20:25]
    rows_by, queries, keys, values, normed_out, active_out, slope_out, sent = refs[25:]

    def prepare():
        me = me_ref[0]
        mine = pl.ds(pl.multiple_of(me * 64, 64), 64)

        for s in range(8):
            owner = lax.rem(me + (8 - s), 8)
            for g in range(4):
                rows_by[owner, 128 * g : 128 * g + 128, :] = held[s][
                    :, TD + 128 * g : TD + 128 * g + 128
                ]
        for b in range(8):
            own_out[:, 128 * b : 128 * b + 128] = rows_by[b, mine, :]

        for s in range(8):
            queries[128 * s : 128 * s + 128, :] = made[s][:, :256]
            keys[128 * s : 128 * s + 128, :] = made[s][:, 256:512]
            values[128 * s : 128 * s + 128, :] = made[s][:, 512:]

    step = pl.program_id(0)
    pl.when(step == 0)(prepare)
    rows = pl.ds(pl.multiple_of(step * 128, 128), 128)
    student = jnp.concatenate([rows_by[b, rows, :] for b in range(8)], axis=1).astype(F32)
    normed = layer_norm(student, gain[...]).astype(BF)
    normed_out[rows, :] = normed
    pre = jnp.dot(normed, widen[...], preferred_element_type=F32)
    half = 0.5 * (1.0 + lax.erf(pre * 0.7071067811865476))
    active = (pre * half).astype(BF)
    active_out[rows, :] = active
    slope_out[rows, :] = half + pre * 0.3989422804014327 * jnp.exp(-0.5 * pre * pre)
    joint[:, :1024] = jnp.dot(active, narrow[...], preferred_element_type=F32).astype(BF)

    spots = lax.broadcasted_iota(jnp.int32, (128, 1024), 1)
    chosen = jnp.where(spots == place[rows, :], 1.0, 0.0).astype(BF)
    query = jnp.dot(chosen, queries[...], preferred_element_type=F32).astype(BF)
    heads = []
    for h in range(2):
        lanes = slice(128 * h, 128 * h + 128)
        scores = lax.dot_general(
            query[:, lanes], keys[:, lanes], LANES, preferred_element_type=F32
        ) * ((TD // TH) ** (-0.5))
        top = jnp.max(scores, axis=-1, keepdims=True)
        num = jnp.exp(scores - top)
        soft = (num * (1.0 / jnp.sum(num, axis=-1, keepdims=True))).astype(BF)
        heads.append(jnp.dot(soft, values[:, lanes], preferred_element_type=F32)[:, :88])
    heads.append(jnp.zeros((128, 80), F32))
    joint[:, 1024:] = jnp.concatenate(heads, axis=1).astype(BF)

    def sending(k, band):
        near = (normed_out, active_out, slope_out)[k]
        band_rows = pl.ds(pl.multiple_of(band * 128, 128), 128)
        return pltpu.make_async_copy(
            near.at[band_rows, :], far[k].at[band_rows, :], sent.at[k, band]
        )

    for k in range(3):
        sending(k, step).start()

    def finish():
        for k in range(3):
            for band in range(4):
                sending(k, band).wait()

    pl.when(step == 3)(finish)


def middle(me, held, made, place, gain, widen, narrow):
    def banded(width):
        return pl.BlockSpec((128, width), lambda i: (i, 0))

    def once(width):
        return pl.BlockSpec((64, width), lambda i: (0, 0))

    return pl.pallas_call(
        middle_body,
        grid=(4,),
        out_shape=[
            jax.ShapeDtypeStruct((512, 1024), BF),
            jax.ShapeDtypeStruct((512, 512), BF),
            jax.ShapeDtypeStruct((512, 512), F32),
            jax.ShapeDtypeStruct((512, 1280), BF),
            jax.ShapeDtypeStruct((64, 1024), BF),
        ],
        in_specs=[SMEM] + [VMEM] * 20,
        out_specs=[HBM, HBM, HBM, banded(1280), once(1024)],
        scratch_shapes=[pltpu.VMEM((8, 512, 128), BF)]
        + [pltpu.VMEM((1024, 256), BF)] * 3
        + [
            pltpu.VMEM((512, 1024), BF),
            pltpu.VMEM((512, 512), BF),
            pltpu.VMEM((512, 512), F32),
            pltpu.SemaphoreType.DMA((3, 4)),
        ],
        compiler_params=pltpu.CompilerParams(vmem_limit_bytes=48 << 20),
        cost_estimate=pl.CostEstimate(
            flops=2 * 512 * 1024 * (1024 + 768),
            bytes_accessed=12_000_000,
            transcendentals=0,
        ),
    )(me, *held, *made, place, gain, widen, narrow)


def loss_body(
    weight, arrived, own, picked, out_far, head_far, back_out, out_full, head_full, arrivals
):
    out_copy = pltpu.make_async_copy(out_far, out_full, arrivals.at[0])
    head_copy = pltpu.make_async_copy(head_far, head_full, arrivals.at[1])
    out_copy.start()
    head_copy.start()
    branch = arrived[0, :, :1024].astype(F32)
    for b in range(1, 8):
        branch += arrived[b, :, :1024].astype(F32)
    outputs = (own[...].astype(F32) + branch).astype(BF)
    joined = jnp.concatenate([arrived[b, :, 1024:].astype(F32)[:, :176] for b in range(8)], axis=1).astype(BF)
    out_copy.wait()
    blended = lax.dot_general(joined, out_full[...], LANES, preferred_element_type=F32)
    targets = (picked[...].astype(F32) + blended).astype(BF).astype(F32)
    head_copy.wait()
    predicted = lax.dot_general(outputs, head_full[...], LANES, preferred_element_type=F32)
    inner = jnp.sum(predicted * targets, axis=-1, keepdims=True)
    inv_pred = lax.rsqrt(jnp.sum(predicted * predicted, axis=-1, keepdims=True) + EPSILON)
    inv_target = lax.rsqrt(jnp.sum(targets * targets, axis=-1, keepdims=True) + EPSILON)
    cosine = inner * inv_pred * inv_target
    row_weight = weight[...]
    slope = (row_weight * cosine * inv_pred * inv_pred) * predicted - (
        row_weight * inv_pred * inv_target
    ) * targets
    back = jnp.dot(slope.astype(BF), head_full[...], preferred_element_type=F32).astype(BF)
    loss = jnp.sum(row_weight * (1.0 - cosine), axis=0, keepdims=True)
    high = loss.astype(BF).astype(F32)
    lane = lax.broadcasted_iota(jnp.int32, (16, 128), 1)
    row = lax.broadcasted_iota(jnp.int32, (16, 128), 0)
    extra = jnp.where(lane == 0, high, jnp.where(lane == 1, loss - high, 0.0))
    extra = jnp.where(row == 0, extra, 0.0).astype(BF)
    for peer in range(8):
        for t in range(32):
            r, c = 16 * (t // 8), 128 * (t % 8)
            back_out[peer, t] = back[r : r + 16, c : c + 128]
        back_out[peer, 32] = extra


def loss_step(weight, arrived, own, picked, out_full, head_full):
    return pl.pallas_call(
        loss_body,
        out_shape=jax.ShapeDtypeStruct((8, 33, 16, 128), BF),
        in_specs=[VMEM] * 4 + [HBM] * 2,
        out_specs=VMEM,
        scratch_shapes=[
            pltpu.VMEM((TD, TD), BF),
            pltpu.VMEM((TD, 1024), BF),
            pltpu.SemaphoreType.DMA((2,)),
        ],
        compiler_params=pltpu.CompilerParams(vmem_limit_bytes=51 << 20),
        cost_estimate=pl.CostEstimate(
            flops=2 * 64 * 1408 * (1408 + 2048), bytes_accessed=10_000_000, transcendentals=0
        ),
    )(weight, arrived, own, picked, out_full, head_full)


def assemble_body(pieces, out_full, head_full):
    for t in range(121):
        r, c = 16 * (t // 11), 128 * (t % 11)
        out_full[r : r + 16, c : c + 128] = pieces[t // 8, 0, t % 8]
    for t in range(88):
        r, c = 16 * (t // 8), 128 * (t % 8)
        head_full[r : r + 16, c : c + 128] = pieces[t // 6, 0, 8 + t % 6]


def assemble(pieces):
    return pl.pallas_call(
        assemble_body,
        grid=(8,),
        out_shape=[jax.ShapeDtypeStruct((TD, TD), BF), jax.ShapeDtypeStruct((TD, 1024), BF)],
        in_specs=[pl.BlockSpec((16, 1, 14, 16, 128), lambda y: (0, y, 0, 0, 0))],
        out_specs=[
            pl.BlockSpec((176, TD), lambda y: (y, 0)),
            pl.BlockSpec((176, 1024), lambda y: (y, 0)),
        ],
        compiler_params=pltpu.CompilerParams(vmem_limit_bytes=56 << 20),
        cost_estimate=pl.CostEstimate(flops=0, bytes_accessed=14_000_000, transcendentals=0),
    )(pieces)


def tail_body(core_ref, back_in, normed, active, slope, narrow, keep, send, loss, back, pre):
    core = core_ref[0]
    for y in range(8):
        for t in range(32):
            r, c = 64 * y + 16 * (t // 8), 128 * (t % 8)
            back[r : r + 16, c : c + 128] = back_in[y, t]
    total = back_in[0, 32].astype(F32)
    for y in range(1, 8):
        total += back_in[y, 32].astype(F32)
    loss[0] = jnp.sum(total)

    def rows_chunk(i, _):
        rows = pl.ds(pl.multiple_of(i * 128, 128), 128)
        got = lax.dot_general(back[rows, :], narrow[...], LANES, preferred_element_type=F32)
        pre[rows, :] = (got * slope[rows, :]).astype(BF)
        return 0

    lax.fori_loop(0, 4, rows_chunk, 0)
    over_rows = (((0,), (0,)), ((), ()))

    def column_chunk(j, _):
        cols = pl.ds(pl.multiple_of(j * 128, 128), 128)
        grad_w = lax.dot_general(
            normed[:, cols], pre[...], over_rows, preferred_element_type=F32
        ).astype(BF)
        grad_n = lax.dot_general(
            back[:, cols], active[...], over_rows, preferred_element_type=F32
        ).astype(BF)

        def put(even, odd):
            for q in range(8):
                target = odd if q % 2 else even
                target[4 * j + q // 2, :16, :] = grad_w[16 * q : 16 * q + 16]
                target[4 * j + q // 2, 16:, :] = grad_n[16 * q : 16 * q + 16]

        pl.when(core == 0)(lambda: put(keep, send))
        pl.when(core == 1)(lambda: put(send, keep))
        return 0

    lax.fori_loop(0, 8, column_chunk, 0)


def tail(core, back, normed, active, slope, narrow):
    half = jax.ShapeDtypeStruct((32, 32, 512), BF)
    return pl.pallas_call(
        tail_body,
        out_shape=[half, half, jax.ShapeDtypeStruct((1,), F32)],
        in_specs=[SMEM] + [VMEM] * 5,
        out_specs=[VMEM, VMEM, SMEM],
        scratch_shapes=[pltpu.VMEM((512, 1024), BF), pltpu.VMEM((512, 512), BF)],
        compiler_params=pltpu.CompilerParams(vmem_limit_bytes=12 << 20),
        cost_estimate=pl.CostEstimate(
            flops=6 * 512 * 1024 * 512, bytes_accessed=8_000_000, transcendentals=0
        ),
    )(core, back, normed, active, slope, narrow)


def on_device(
    teacher_in,
    teacher_gain,
    teacher_qkv,
    teacher_out,
    student_in,
    student_gain,
    widen_weight,
    narrow_weight,
    target_head,
    positions,
    counts,
):
    me = lax.axis_index("mp")
    picked = positions[0]
    live_count = counts[0]

    rows = student_in[0][picked]
    packed = jnp.concatenate([rows[128 * g : 128 * g + 128] for g in range(4)], axis=1)
    held = ring(jnp.concatenate([teacher_in[0], packed], axis=1))

    at = lax.axis_index(("z", "c"))
    mine = jnp.concatenate(
        [
            lax.dynamic_index_in_dim(to_tiles(teacher_out, 8), at, 0, False),
            lax.dynamic_index_in_dim(to_tiles(target_head, 6), at, 0, False),
        ]
    )
    pieces = lax.all_gather(mine, ("z", "c", "mp"), axis=0)
    out_full, head_full = assemble(pieces.reshape(16, 8, 14, 16, 128))

    here = jnp.reshape(me, (1,)).astype(jnp.int32)
    place = ((me - picked // 128) % 8) * 128 + picked % 128
    own_place = lax.dynamic_slice_in_dim(place, me * 64, 64, 0).reshape(64, 1)
    made = [None] * 8
    own_patches = jnp.zeros((64, TD), BF)
    for s in (0, 1, 7, 2, 6, 3, 5, 4):
        made[s], own_patches = project(
            held[s], teacher_gain.reshape(1, -1), teacher_qkv, own_place - 128 * s, own_patches
        )
    normed_rows, activity, slope_pre, joint, own_rows = middle(
        here,
        held,
        made,
        place.reshape(512, 1),
        student_gain.reshape(1, -1),
        widen_weight,
        narrow_weight,
    )
    arrived = lax.all_to_all(joint.reshape(8, 64, 1280), "mp", 0, 0, tiled=True)

    slot = me * 64 + jnp.arange(64, dtype=jnp.int32)
    row_weight = jnp.where(slot < live_count, 1.0 / live_count.astype(F32), jnp.zeros((), F32))
    back_own = loss_step(
        row_weight.reshape(64, 1), arrived, own_rows, own_patches, out_full, head_full
    )
    back = lax.all_to_all(back_own, "mp", 0, 0, tiled=True)

    core = jnp.reshape(lax.axis_index("c"), (1,)).astype(jnp.int32)
    keep, send, image_loss = tail(core, back, normed_rows, activity, slope_pre, narrow_weight)
    other = lax.ppermute(send, "c", [(0, 1), (1, 0)])
    kept = (keep.astype(F32) + other.astype(F32)).astype(BF)
    kept = lax.all_to_all(kept, ("z", "x"), 0, 0, tiled=True)
    total = jnp.sum(kept.astype(F32), axis=0)
    return (total[:16], total[16:], image_loss)


def solution(mesh):
    grid = Mesh(mesh.devices.reshape(8, 4, 2, 8), ("z", "x", "c", "mp"))
    placed = (
        P(DP, "mp", None),
        P(),
        P(None, "mp", None),
        P("mp", None),
        P(DP, None, "mp"),
        P(),
        P(None, "mp"),
        P("mp", None),
        P("mp", None),
        P(DP, None),
        P(DP),
    )
    return jax.shard_map(
        on_device,
        mesh=grid,
        in_specs=placed,
        out_specs=(P(DP, "mp"), P(DP, "mp"), P(DP)),
        check_vma=False,
    )
```
